256 devices in a mesh: gx: 32 (over x, z), gy: 8 (over y, core).
Axes of the slice: x: 4, y: 4, z: 8, core: 2. Of those that a mesh axis runs over, the one named last changes fastest.
Arguments:
- velocity: float32 [3, 16, 4096, 1024], P(None, None, 'gx', 'gy'), may hold values from -6 to 6
- inv_x: float32 [4096, 128], P('gx'), as said below
- inv_y: float32 [1024, 128], P('gy'), as said below
- spike_x: float32 [4096, 2], P('gx'), as said below
- spike_y: float32 [1024, 2], P('gy'), as said below
- marker_force: bfloat16 [3, 524288], P(None, ('gx', 'gy')), may hold values from -6 to 6
- marker_kernel: bfloat16 [524288, 128], P(('gx', 'gy')), may hold values from 0 to 1
- marker_owner: int32 [524288, 1], P(('gx', 'gy')), may hold values from 0 to 31; in each aligned block of 2048 rows (0 to 2047, 2048 to 4095, ...) at most 128 rows name the same one
- marker_row: int32 [524288], P(('gx', 'gy')), may hold values from 0 to 2047
Outputs:
- section_velocity: float32 [3, 16, 4096, 1024], P(None, None, 'gx', 'gy')
The draws below stay inside these ranges and needn't reach their ends.
Inputs may be any that keep to these rules, and one draw needn't show every extreme that they name: `marker_owner`: among the 2048 marker slots of one device, no owner is named more than 128 times, a bound that some block reaches; every owner is named somewhere. `inv_x`: one block for each streamwise block of cells. `inv_y`: one block for each spanwise block of cells. `spike_x`: two columns for each streamwise block of cells. `spike_y`: two columns for each spanwise block of cells.
All inputs are finite; a program needn't handle non-finite values.
Results may differ from the reference program's by a relative error of at most 0.00046.
Values may be sent and summed in bfloat16 or wider, within the bound.
A program may use at most 128 MiB of HBM per device.

```python
import math
import jax
import jax.numpy as jnp
import numpy as np
from jax import lax

NZ = 16
CX = 128
CY = 128
M_DEV = 2048
NX = 4096
NY = 1024
MARKERS = 524288
CAP = 128
N_GX = 32
N_GY = 8


def block_draw(key, rows, width):
    first, second = jax.random.split(key)
    local = lax.broadcasted_iota(jnp.int32, (rows, width), 0) % width
    column = lax.broadcasted_iota(jnp.int32, (rows, width), 1)
    spread = 0.5 / width ** 0.5
    off = jax.random.normal(first, (rows, width), jnp.float32) * spread
    main = jax.random.uniform(second, (rows, width), jnp.float32, 0.8, 1.2)
    return jnp.where(local == column, main, off)


def spike_draw(key, rows, width):
    first, second, third = jax.random.split(key, 3)
    local = lax.broadcasted_iota(jnp.int32, (rows, 2), 0) % width
    column = lax.broadcasted_iota(jnp.int32, (rows, 2), 1)
    body_part = jax.random.normal(first, (rows, 2), jnp.float32) * 0.4
    keep = jax.random.uniform(second, (rows, 2), jnp.float32, 0.92, 0.99)
    cross = jax.random.uniform(third, (rows, 2), jnp.float32, -0.03, 0.03)
    tail = jnp.where(local - (width - 2) == column, keep, cross)
    return jnp.where(local >= width - 2, tail, body_part)


def draw_inv_x(key, part):
    return block_draw(jax.random.fold_in(key, 11), NX, CX)


def draw_inv_y(key, part):
    return block_draw(jax.random.fold_in(key, 12), NY, CY)


def draw_spike_x(key, part):
    return spike_draw(jax.random.fold_in(key, 13), NX, CX)


def draw_spike_y(key, part):
    return spike_draw(jax.random.fold_in(key, 14), NY, CY)


def plant(entries, stream_key, least, largest):
    spot = [jax.random.randint(jax.random.fold_in(stream_key, axis), (), 0, length) for axis, length in enumerate(entries.shape)]
    longest = entries.shape.index(max(entries.shape))
    next_to = spot[:longest] + [(spot[longest] + 1) % entries.shape[longest]] + spot[longest + 1:]
    return entries.at[tuple(spot)].set(least).at[tuple(next_to)].set(largest)


def shard_levels(own_key, extent, pieces, smallest, top_value):
    def one(position, shards_of):
        draws = jax.random.uniform(jax.random.fold_in(jax.random.fold_in(own_key, 6), position), (shards_of,), jnp.float32, smallest / len(pieces), top_value / len(pieces))
        return jnp.repeat(jnp.exp(draws), extent[position] // shards_of).reshape((-1,) + (1,) * (len(extent) - position - 1))

    gain = one(*pieces[0])
    for cut in pieces[1:]:
        gain = gain * one(*cut)
    return gain


def deal_out(own_key, own, number, rows, count, top, bound, skew):
    ranking = jax.random.permutation(own_key, count)
    heavy_load, common = shares(count, rows * top, bound, skew, True), shares(count, rows * top, bound, skew, False)
    places = jnp.arange(count)

    def named(lengths, turn):
        used = int((lengths > 0).sum())
        fixed = max(1, used // 4)
        shifted = fixed + (places - fixed + turn * (used - fixed)) % max(1, count - fixed)
        return jnp.zeros((count,), jnp.int32).at[ranking[jnp.where(places < fixed, places, shifted)]].set(jnp.asarray(lengths, jnp.int32))

    lengths = jnp.where(number % 4 == 0, named(heavy_load, number // 4), named(common, number - number // 4 - 1))
    mixed = jax.random.permutation(jax.random.fold_in(own, 3), count)
    source_of, taker = mixed[0:count // 2 * 2:2], mixed[1:count // 2 * 2:2]
    room = jnp.minimum(lengths[source_of] - 1, bound - lengths[taker]) // 2
    room = jnp.where((source_of == ranking[0]) | (taker == ranking[0]) | (lengths[taker] == 0), 0, jnp.maximum(room, 0))
    shifted = jax.random.randint(jax.random.fold_in(own, 4), (count // 2,), 0, 1 << 20) % (room + 1)
    lengths = lengths.at[source_of].add(-shifted).at[taker].add(shifted)
    items = jnp.searchsorted(jnp.cumsum(lengths), jnp.arange(rows * top), side="right").astype(jnp.int32)
    listing = items.reshape(top, rows).T
    listing = listing[jax.random.permutation(jax.random.fold_in(own, 1), rows)]
    turn = jax.random.randint(jax.random.fold_in(own, 2), (rows, 1), 0, top)
    return jnp.take_along_axis(listing, (jnp.arange(top)[None, :] + turn) % top, axis=1)


def shares(amount, total, reach, lean, full):
    loads = [(1 << 20) // math.isqrt(rank ** lean) + 1 for rank in range(1, amount + 1)]
    largest = reach if full else min(reach, max(-(-total // amount), total * loads[0] // sum(loads)))
    least = 1 if total - largest >= amount - 1 else 0
    counts, rest = [largest] + [least] * (amount - 1), total - largest - least * (amount - 1)
    while rest > 0:
        candidates = [i for i in range(1, amount) if counts[i] < largest] or [i for i in range(1, amount) if counts[i] < reach]
        whole, budget = sum([loads[i] for i in candidates]), rest
        for i in candidates:
            extra = min(reach - counts[i], max(1, budget * loads[i] // whole), rest)
            counts[i] = counts[i] + extra
            rest = rest - extra
    return np.array(counts)


def noise(stream_key, extent, deviation, most, cuts=(), held_as=jnp.bfloat16):
    level = shard_levels(stream_key, extent, cuts, -0.22, 0.18) if cuts else 1.0
    values = jax.random.normal(stream_key, extent, jnp.float32) * deviation * level
    return jnp.minimum(jnp.maximum(values, -most), most).astype(held_as)


def setup_inputs(seed: int = 0) -> dict:
    arg_keys = jax.random.split(jax.random.key(seed), 10)
    velocity = noise(arg_keys[0], (3, NZ, NX, NY), 1.0, 6.0, ((2, 32), (3, 8)), jnp.float32)
    inv_x = draw_inv_x(jax.random.fold_in(arg_keys[9], 71), 0)
    inv_y = draw_inv_y(jax.random.fold_in(arg_keys[9], 71), 0)
    spike_x = draw_spike_x(jax.random.fold_in(arg_keys[9], 71), 0)
    spike_y = draw_spike_y(jax.random.fold_in(arg_keys[9], 71), 0)
    marker_force = noise(arg_keys[5], (3, MARKERS), 1.0, 6.0, ((1, 256),))
    marker_kernel = jnp.clip(1.0 * jax.random.uniform(arg_keys[6], (MARKERS, CY), jnp.float32) ** shard_levels(arg_keys[6], (MARKERS, CY), ((0, 256),), -0.2, 0.2), 0.0, 1.0).astype(jnp.bfloat16)
    marker_owner_keys = jax.random.split(jax.random.fold_in(arg_keys[7], 1), MARKERS // M_DEV)
    marker_owner_turns = jax.random.permutation(jax.random.fold_in(arg_keys[7], 3), MARKERS // M_DEV)
    marker_owner = jax.vmap(lambda own, number: deal_out(jax.random.fold_in(arg_keys[7], 2), own, number, M_DEV, N_GX, 1, CAP, 2))(marker_owner_keys, marker_owner_turns).reshape((MARKERS, 1))
    marker_row = plant(jax.random.randint(arg_keys[8], (MARKERS,), 0, NZ * CX), jax.random.fold_in(arg_keys[8], 1), 0, (NZ * CX) - 1).astype(jnp.int32)
    return {"velocity": velocity, "inv_x": inv_x, "inv_y": inv_y, "spike_x": spike_x, "spike_y": spike_y, "marker_force": marker_force, "marker_kernel": marker_kernel, "marker_owner": marker_owner, "marker_row": marker_row}


HIGH = lax.Precision.HIGHEST


def stencil(padded, axis):
    size = padded.shape[axis] - 4
    def cut(start):
        return lax.slice_in_dim(padded, start, start + size, axis=axis)
    return (7.0 / 9.0) * (cut(3) - cut(1)) + (1.0 / 36.0) * (cut(4) - cut(0))


def chain(maps, parts):
    def step(state, item):
        pmap, part = item
        new_state = jnp.einsum('ab,czbl->czal', pmap, state, precision=HIGH) + part
        return new_state, state
    start = jnp.zeros(parts.shape[1:], jnp.float32)
    final, before = lax.scan(step, start, (maps, parts))
    return before


def reference(velocity, inv_x, inv_y, spike_x, spike_y, marker_force, marker_kernel, marker_owner, marker_row):
    padded = jnp.pad(velocity, ((0, 0), (0, 0), (2, 2), (2, 2)))
    rx = stencil(padded[:, :, :, 2:-2], 2)
    ry = stencil(padded[:, :, 2:-2, :], 3)

    blocks_x = inv_x.reshape(N_GX, CX, CX)
    cols_x = spike_x.reshape(N_GX, CX, 2)
    vx = jnp.einsum('dij,czdjy->czdiy', blocks_x, rx.reshape(3, NZ, N_GX, CX, NY), precision=HIGH)
    qx = jnp.moveaxis(vx[:, :, :, CX - 2:, :], 2, 0)
    sx = chain(cols_x[:, CX - 2:, :], qx)
    dx = (vx + jnp.einsum('dia,dczay->czdiy', cols_x, sx, precision=HIGH)).reshape(3, NZ, NX, NY)

    blocks_y = inv_y.reshape(N_GY, CY, CY)
    cols_y = spike_y.reshape(N_GY, CY, 2)
    vy = jnp.einsum('dij,czxdj->czxdi', blocks_y, ry.reshape(3, NZ, NX, N_GY, CY), precision=HIGH)
    qy = jnp.transpose(vy[..., CY - 2:], (3, 0, 1, 4, 2))
    sy = chain(cols_y[:, CY - 2:, :], qy)
    dy = (vy + jnp.einsum('dia,dczax->czxdi', cols_y, sy, precision=HIGH)).reshape(3, NZ, NX, NY)

    owner_all = marker_owner[:, 0].reshape(N_GX, N_GY, M_DEV)
    row_all = marker_row.reshape(N_GX, N_GY, M_DEV)
    force_all = marker_force.reshape(3, N_GX, N_GY, M_DEV)
    kernel_all = marker_kernel.reshape(N_GX, N_GY, M_DEV, CY)
    columns = []
    for column in range(N_GY):
        owner = owner_all[:, column].reshape(-1).astype(jnp.int32)
        row = row_all[:, column].reshape(-1).astype(jnp.int32)
        force_col = force_all[:, :, column].reshape(3, -1)
        kernel_col = kernel_all[:, column].reshape(-1, CY)
        tiles = (force_col.T[:, :, None].astype(jnp.float32) * kernel_col[:, None, :].astype(jnp.float32)).astype(jnp.bfloat16)
        tiles = lax.optimization_barrier(tiles).astype(jnp.float32)
        index = (row // CX) * NX + owner * CX + row % CX
        summed = jnp.zeros((NZ * NX, 3, CY), jnp.float32).at[index].add(tiles)
        columns.append(jnp.transpose(summed, (1, 0, 2)))
    force = jnp.concatenate(columns, axis=2).reshape(3, NZ, NX, NY)

    return velocity + 0.5 * (force - velocity[0:1] * dx - velocity[1:2] * dy)
```

```python
import functools

import jax
import jax.numpy as jnp
from jax import lax
from jax.experimental import pallas as pl
from jax.experimental.pallas import tpu as pltpu
from jax.sharding import PartitionSpec as P

HIGH = lax.Precision.HIGHEST
MESH = pl.DeviceIdType.MESH
F32, BF16 = jnp.float32, jnp.bfloat16
N = 128
CAP = 128
BLOCK = CAP + 16
NEAR, FAR = 7.0 / 9.0, 1.0 / 36.0


def iota(shape, dim):
    return lax.broadcasted_iota(jnp.int32, shape, dim)


def mm(a, b):
    return jnp.dot(a, b, preferred_element_type=F32)


def mm_nt(a, b, precision=None):
    return lax.dot_general(a, b, (((1,), (1,)), ((), ())), precision=precision, preferred_element_type=F32)


def split(a):
    hi = a.astype(BF16)
    return hi, (a - hi.astype(F32)).astype(BF16)


def inner_stencil(cell, row):
    gap = cell - row
    return jnp.where(gap == 1, NEAR, 0.0) - jnp.where(gap == -1, NEAR, 0.0) + jnp.where(gap == 2, FAR, 0.0) - jnp.where(gap == -2, FAR, 0.0)


def outer_stencil(row, column, first):
    which = column - first
    low2 = jnp.where((which == 0) & (row == 0), -FAR, 0.0)
    low1 = jnp.where((which == 1) & (row == 0), -NEAR, 0.0) + jnp.where((which == 1) & (row == 1), -FAR, 0.0)
    high1 = jnp.where((which == 2) & (row == N - 1), NEAR, 0.0) + jnp.where((which == 2) & (row == N - 2), FAR, 0.0)
    high2 = jnp.where((which == 3) & (row == N - 1), FAR, 0.0)
    return low2 + low1 + high1 + high2


def last_rows(inverse, spike_t):
    sub, lane = iota((N, N), 0), iota((N, N), 1)
    inner_t = inner_stencil(sub, lane)
    spread = [
        mm_nt(inner_t, jnp.broadcast_to(inverse[N - 2 + a : N - 1 + a, :], (N, N)), HIGH) for a in range(2)
    ]
    outer = jnp.dot(inverse[N - 8 :, :], outer_stencil(sub, lane, 0), precision=HIGH, preferred_element_type=F32)
    part, column = iota((2, N), 0), iota((2, N), 1)
    place = iota((1, N), 1)
    rows = []
    for a in range(2):
        row = outer[6 + a : 7 + a, :]
        for b in range(2):
            picked = jnp.where((part == b) & (column == N - 2 + a), spike_t, 0.0)
            value = jnp.sum(jnp.sum(picked, axis=1, keepdims=True), axis=0, keepdims=True)
            row = row + jnp.where(place == 4 + b, value, 0.0)
        rows.append(row)
    return spread, rows


def pack_kernel(groups, v_hbm, gx_ref, gy_ref, wx_ref, wy_ref, f_ref, k_ref, own_ref, row_ref,
                mk_ref, mx_ref, my_ref, v_ref, wide_ref, pos_ref, acc_ref, sem):
    depth = v_hbm.shape[1]
    chunks = own_ref.shape[0]
    fetch = pltpu.make_async_copy(v_hbm, v_ref, sem)
    fetch.start()

    sub, lane = iota((N, N), 0), iota((N, N), 1)
    upto = jnp.concatenate([(sub <= lane).astype(BF16), jnp.ones((N, N), BF16)], axis=1)
    name = iota((groups, N), 0)
    before = jnp.zeros((groups, N), F32)
    for k in range(chunks):
        owner = own_ref[k : k + 1, :]
        hit = name == owner
        counted = mm(hit.astype(F32).astype(BF16), upto)
        rank = counted[:, :N] + before - 1.0
        before = before + counted[:, N:]
        place = jnp.sum(jnp.where(hit, rank, 0.0), axis=0, keepdims=True)
        pos_ref[0:1, k * N : (k + 1) * N] = owner.astype(F32)
        pos_ref[1:2, k * N : (k + 1) * N] = place

        cell = row_ref[k : k + 1, :]
        plane = cell // N
        upper = plane >= depth // 2
        three = f_ref[:, k * N : (k + 1) * N].astype(F32)
        facts = jnp.concatenate(
            [
                jnp.where(upper, 0.0, three),
                jnp.where(upper, three, 0.0),
                (plane % (depth // 2)).astype(F32),
                (cell % N).astype(F32),
            ],
            axis=0,
        )
        wide_ref[k * N : (k + 1) * N, 0:N] = k_ref[k * N : (k + 1) * N, :]
        wide_ref[k * N : (k + 1) * N, N:] = jnp.tile(facts, (N // 8, 1)).T.astype(BF16)

    per = min(groups, 4)
    slot = iota((CAP, 1), 0).astype(F32).astype(BF16)
    turn = iota((CAP, N), 1) // 8

    @pl.loop(0, groups // per)
    def _(step):
        owner, place = pos_ref[0:1, :], pos_ref[1:2, :]
        picks = []
        for i in range(per):
            group = step * per + i
            mine = jnp.where(owner == group.astype(F32), place, -1.0).astype(BF16)
            picks.append(jnp.where(mine == slot, jnp.ones((), BF16), jnp.zeros((), BF16)))
        rows = mm(jnp.concatenate(picks, axis=0), wide_ref[...])
        for i in range(per):
            group = step * per + i
            part = rows[i * CAP : (i + 1) * CAP]
            mk_ref[group, 0:CAP, :] = part[:, :N].astype(BF16)
            facts_t = part[:, N:].T[0:8, :]
            mk_ref[group, CAP:, :] = jnp.concatenate([facts_t, jnp.zeros((8, N), F32)], axis=0).astype(BF16)

    (sx0, sx1), (cx0, cx1) = last_rows(gx_ref[...], wx_ref[...])
    (sy0, sy1), (cy0, cy1) = last_rows(gy_ref[...], wy_ref[...])
    kind = lane % 8
    base = jnp.where(kind == 0, sy0, jnp.where(kind == 1, sy1, 0.0))
    for i, cell in enumerate((0, 1, N - 2, N - 1)):
        base = base + jnp.where((kind == 2 + i) & (sub == cell), 1.0, 0.0)
    base_hi, base_lo = (p.astype(F32) for p in split(base))
    fetch.wait()
    acc_ref[...] = jnp.zeros_like(acc_ref)

    @pl.loop(0, depth)
    def _(z):
        for c in range(3):
            block = v_ref[c, z]
            mx_ref[z, c] = jnp.concatenate(
                [
                    jnp.sum(block * sx0, axis=0, keepdims=True),
                    jnp.sum(block * sx1, axis=0, keepdims=True),
                    block[0:2],
                    block[N - 2 :],
                    cx0,
                    cx1,
                ],
                axis=0,
            )
        mine = lane // 8 == z
        hi = jnp.where(mine, base_hi, 0.0).astype(BF16)
        lo = jnp.where(mine, base_lo, 0.0).astype(BF16)
        v_hi, v_lo = split(v_ref[:, z].reshape(3 * N, N))
        acc_ref[...] += mm(jnp.concatenate([v_hi, v_lo], axis=1), jnp.concatenate([hi, hi], axis=0)) + mm(v_hi, lo)

    kind_row = sub % 8
    for c in range(3):
        lines = acc_ref[c * N : (c + 1) * N, :].T
        lines = jnp.where(kind_row == 6, cy0, jnp.where(kind_row == 7, cy1, lines))
        my_ref[:, c] = lines.reshape(depth, 8, N)


def chain(count, got, reply):
    zero = jnp.zeros(got.shape[1:3] + (1, N), F32)

    def one(d, carry):
        s0, s1, low2, low1 = carry
        here = got[d]
        after = got[jnp.minimum(d + 1, count - 1)]
        more = (d + 1 < count).astype(F32)
        high1, high2 = after[:, :, 2:3, :] * more, after[:, :, 3:4, :] * more
        reply[d] = jnp.concatenate([s0, s1, low2, low1, high1, high2, zero, zero], axis=2)
        new = []
        for a in range(2):
            weight = here[:, :, 6 + a : 7 + a, :]
            total = here[:, :, a : a + 1, :]
            for k, value in enumerate((low2, low1, high1, high2, s0, s1)):
                total = total + weight[:, :, :, k : k + 1] * value
            new.append(total)
        return new[0], new[1], here[:, :, 4:5, :], here[:, :, 5:6, :]

    lax.fori_loop(0, count, one, (zero, zero, zero, zero))


def comm_kernel(nx, ny, mk_ref, mx_ref, my_ref, got_mk, ex_ref, ey_ref,
                got_x, got_y, reply_x, reply_y, send_m, recv_m, send_x, recv_x, send_y, recv_y,
                back_send_x, back_recv_x, back_send_y, back_recv_y, own_sem):
    gx, gy = lax.axis_index("gx"), lax.axis_index("gy")
    depth = mx_ref.shape[0]
    sx, sy = min(depth, nx), min(depth, ny)
    zx, zy = depth // sx, depth // sy

    barrier = pltpu.get_barrier_semaphore()

    @pl.loop(1, nx)
    def _(i):
        pl.semaphore_signal(barrier, inc=1, device_id=(lax.rem(gx + i, nx), gy), device_id_type=MESH)

    @pl.loop(1, ny)
    def _(i):
        pl.semaphore_signal(barrier, inc=1, device_id=(gx, lax.rem(gy + i, ny)), device_id_type=MESH)

    pl.semaphore_wait(barrier, nx + ny - 2)

    def out_x(to, origin):
        return pltpu.make_async_remote_copy(
            src_ref=mx_ref.at[pl.ds(to * zx, zx)], dst_ref=got_x.at[origin],
            send_sem=send_x.at[to], recv_sem=recv_x.at[origin],
            device_id=(to, gy), device_id_type=MESH)

    def out_y(to, origin):
        return pltpu.make_async_remote_copy(
            src_ref=my_ref.at[pl.ds(to * zy, zy)], dst_ref=got_y.at[origin],
            send_sem=send_y.at[to], recv_sem=recv_y.at[origin],
            device_id=(gx, to), device_id_type=MESH)

    def out_m(to, origin):
        return pltpu.make_async_remote_copy(
            src_ref=mk_ref.at[to], dst_ref=got_mk.at[origin],
            send_sem=send_m.at[to], recv_sem=recv_m.at[origin],
            device_id=(to, gy), device_id_type=MESH)

    def back_x(to, origin):
        return pltpu.make_async_remote_copy(
            src_ref=reply_x.at[to], dst_ref=ex_ref.at[pl.ds(origin * zx, zx)],
            send_sem=back_send_x.at[to], recv_sem=back_recv_x.at[origin],
            device_id=(to, gy), device_id_type=MESH)

    def back_y(to, origin):
        return pltpu.make_async_remote_copy(
            src_ref=reply_y.at[to], dst_ref=ey_ref.at[pl.ds(origin * zy, zy)],
            send_sem=back_send_y.at[to], recv_sem=back_recv_y.at[origin],
            device_id=(gx, to), device_id_type=MESH)

    @pl.loop(0, sx)
    def _(i):
        to = lax.rem(gx + i, sx)

        @pl.when(to != gx)
        def _():
            out_x(to, gx).start()

    @pl.loop(1, ny)
    def _(i):
        out_y(lax.rem(gy + i, ny), gy).start()

    @pl.loop(1, nx)
    def _(i):
        out_m(lax.rem(gx + i, nx), gx).start()

    own = pltpu.make_async_copy(mk_ref.at[gx], got_mk.at[gx], own_sem)
    own.start()

    @pl.when(gx < sx)
    def _():
        got_x[gx] = mx_ref[pl.ds(gx * zx, zx)]

        @pl.loop(1, nx)
        def _(i):
            out_x(gx, lax.rem(gx + i, nx)).wait_recv()

        chain(nx, got_x, reply_x)

        @pl.loop(1, nx)
        def _(i):
            back_x(lax.rem(gx + i, nx), gx).start()

        ex_ref[pl.ds(gx * zx, zx)] = reply_x[gx]

    got_y[gy] = my_ref[pl.ds(gy * zy, zy)]

    @pl.loop(1, ny)
    def _(i):
        out_y(gy, lax.rem(gy + i, ny)).wait_recv()

    chain(ny, got_y, reply_y)

    @pl.loop(1, ny)
    def _(i):
        back_y(lax.rem(gy + i, ny), gy).start()

    ey_ref[pl.ds(gy * zy, zy)] = reply_y[gy]

    @pl.loop(1, ny)
    def _(i):
        other = lax.rem(gy + i, ny)
        out_y(other, gy).wait_send()
        back_y(other, gy).wait_send()
        back_y(gy, other).wait_recv()

    @pl.loop(0, sx)
    def _(i):
        other = lax.rem(gx + i, sx)

        @pl.when(other != gx)
        def _():
            out_x(other, gx).wait_send()
            back_x(gx, other).wait_recv()

    @pl.when(gx < sx)
    def _():
        @pl.loop(1, nx)
        def _(i):
            back_x(lax.rem(gx + i, nx), gx).wait_send()

    @pl.loop(1, nx)
    def _(i):
        other = lax.rem(gx + i, nx)
        out_m(other, gx).wait_send()
        out_m(gx, other).wait_recv()

    own.wait()


def weights(inverse, spike_t):
    sub, lane = iota((N, N), 0), iota((N, N), 1)
    inner = jnp.dot(inverse, inner_stencil(lane, sub), precision=HIGH, preferred_element_type=F32)
    outer = jnp.dot(inverse, outer_stencil(sub, lane % 8, 2), precision=HIGH, preferred_element_type=F32)
    spikes = jnp.tile(jnp.concatenate([spike_t, jnp.zeros((6, N), F32)], axis=0), (N // 8, 1)).T
    return inner, outer + spikes


def final_kernel(got_mk, ex_ref, ey_ref, v_ref, gx_ref, gy_ref, wx_ref, wy_ref, out_ref,
                 force_ref, tile_ref, pick_ref, left_x, left_ex, right_y, right_ey, ext_y):
    sources = got_mk.shape[0]
    step = pl.program_id(0)
    half = ex_ref.shape[0] // 2
    sub, lane = iota((N, N), 0), iota((N, N), 1)

    @pl.when(step == 0)
    def _():
        inner, cols = weights(gx_ref[...], wx_ref[...])
        hi, lo = split(inner)
        left_x[0:N, 0:N], left_x[0:N, N:] = hi, hi
        left_x[N:, 0:N], left_x[N:, N:] = lo, lo
        hi, lo = split(cols)
        left_ex[0:N], left_ex[N:] = hi, lo
        inner, cols = weights(gy_ref[...], wy_ref[...])
        hi, lo = split(inner.T)
        right_y[0:N, 0:N], right_y[0:N, N:] = hi, lo
        right_y[N:, 0:N], right_y[N:, N:] = hi, lo
        hi, lo = split(cols.T)
        right_ey[0:N, 0:N], right_ey[0:N, N:] = hi, lo
        right_ey[N:, 0:N], right_ey[N:, N:] = hi, lo
        for c in range(3):
            hi, lo = split(ey_ref[:, c].reshape(8 * 2 * half, N).T)
            ext_y[c * N : (c + 1) * N, 0:N], ext_y[c * N : (c + 1) * N, N:] = hi, lo

        @pl.loop(0, sources)
        def _(s):
            facts = got_mk[s, CAP:, :].astype(F32)
            columns = jnp.tile(facts[0:8], (N // 8, 1)).T
            rows = got_mk[s, 0:CAP, :].astype(F32)
            at = pl.ds(pl.multiple_of(s * CAP, CAP), CAP)
            for k in range(6):
                tile_ref[at, k * N : (k + 1) * N] = (rows * columns[:, k : k + 1]).astype(BF16)
            x_slot = iota((N, 1), 0).astype(F32).astype(BF16)
            for zz in range(half):
                mine = jnp.where(facts[6:7] == float(zz), facts[7:8], -1.0).astype(BF16)
                pick_ref[zz * N : (zz + 1) * N, at] = jnp.where(mine == x_slot, jnp.ones((), BF16), jnp.zeros((), BF16))

        rows = min(4, half) * N

        @pl.loop(0, half * N // rows)
        def _(r):
            at = pl.ds(pl.multiple_of(r * rows, rows), rows)
            for n in range(3):
                force_ref[at, n * 2 * N : (n + 1) * 2 * N] = mm(pick_ref[at, :], tile_ref[:, n * 2 * N : (n + 1) * 2 * N])

    zs = [step, step + half]
    vs = [[v_ref[c, h, 0] for c in range(3)] for h in range(2)]
    parts = [[split(v) for v in line] for line in vs]
    wide = jnp.concatenate([jnp.concatenate([hi, lo], axis=0) for line in parts for hi, lo in line], axis=1)
    ends = []
    for h in range(2):
        for c in range(3):
            hi, lo = split(ex_ref[zs[h], c])
            ends.append(jnp.concatenate([hi.astype(F32), lo.astype(F32)], axis=0).astype(BF16))
    ends = jnp.concatenate(ends, axis=1)
    both = mm(left_x[...], wide) + mm(left_ex[:, 0:16], ends)
    dx_all = both[:N] + both[N:]
    for h in range(2):
        tall = jnp.concatenate([jnp.concatenate([hi, lo], axis=1) for hi, lo in parts[h]], axis=0)
        mine = iota((2 * N, 2 * N), 0) % N // 8 == zs[h]
        right_ext = jnp.where(mine, right_ey[...].astype(F32), 0.0).astype(BF16)
        both = mm(tall, right_y[...]) + mm(ext_y[...], right_ext)
        dy_all = both[:, :N] + both[:, N:]
        at = pl.ds(pl.multiple_of(step * N, N), N)
        for c in range(3):
            k = h * 3 + c
            dx, dy = dx_all[:, k * N : (k + 1) * N], dy_all[c * N : (c + 1) * N]
            force = force_ref[at, k * N : (k + 1) * N]
            out_ref[c, h, 0] = vs[h][c] + 0.5 * (force - vs[h][0] * dx - vs[h][1] * dy)


def local(nx, ny, velocity, inv_x, inv_y, spike_x, spike_y, marker_force, marker_kernel, marker_owner, marker_row):
    depth = velocity.shape[1]
    slots = marker_row.shape[0]
    wx, wy = spike_x.T, spike_y.T
    vmem, anywhere = pl.BlockSpec(memory_space=pltpu.VMEM), pl.BlockSpec(memory_space=pl.ANY)
    lines = jax.ShapeDtypeStruct((depth, 3, 8, N), F32)
    blocks = jax.ShapeDtypeStruct((nx, BLOCK, N), BF16)
    limit = 48 * 1024 * 1024
    mk, mx, my = pl.pallas_call(
        functools.partial(pack_kernel, nx),
        out_shape=(blocks, lines, lines),
        in_specs=[anywhere] + [vmem] * 8,
        out_specs=(vmem, vmem, vmem),
        scratch_shapes=[
            pltpu.VMEM(velocity.shape, F32),
            pltpu.VMEM((slots, 2 * N), BF16),
            pltpu.VMEM((8, slots), F32),
            pltpu.VMEM((3 * N, N), F32),
            pltpu.SemaphoreType.DMA,
        ],
        compiler_params=pltpu.CompilerParams(vmem_limit_bytes=limit),
        name="pack",
    )(velocity, inv_x, inv_y, wx, wy, marker_force, marker_kernel,
      marker_owner.reshape(slots // N, N), marker_row.reshape(slots // N, N))

    sx, sy = min(depth, nx), min(depth, ny)
    dma = pltpu.SemaphoreType.DMA
    got, ex, ey = pl.pallas_call(
        functools.partial(comm_kernel, nx, ny),
        out_shape=(blocks, lines, lines),
        in_specs=[anywhere, vmem, vmem],
        out_specs=(anywhere, vmem, vmem),
        scratch_shapes=[
            pltpu.VMEM((nx, depth // sx, 3, 8, N), F32),
            pltpu.VMEM((ny, depth // sy, 3, 8, N), F32),
            pltpu.VMEM((nx, depth // sx, 3, 8, N), F32),
            pltpu.VMEM((ny, depth // sy, 3, 8, N), F32),
            dma((nx,)), dma((nx,)), dma((sx,)), dma((nx,)), dma((ny,)), dma((ny,)),
            dma((nx,)), dma((sx,)), dma((ny,)), dma((ny,)), dma,
        ],
        compiler_params=pltpu.CompilerParams(vmem_limit_bytes=limit, collective_id=0, has_side_effects=True),
        name="exchange",
    )(mk, mx, my)

    half = depth // 2
    plane = pl.BlockSpec((3, 2, 1, N, N), lambda i: (0, 0, i, 0, 0))
    out = pl.pallas_call(
        final_kernel,
        grid=(half,),
        out_shape=jax.ShapeDtypeStruct((3, 2, half, N, N), F32),
        in_specs=[vmem, vmem, vmem, plane] + [vmem] * 4,
        out_specs=plane,
        scratch_shapes=[
            pltpu.VMEM((half * N, 6 * N), F32),
            pltpu.VMEM((nx * CAP, 6 * N), BF16),
            pltpu.VMEM((half * N, nx * CAP), BF16),
            pltpu.VMEM((2 * N, 2 * N), BF16),
            pltpu.VMEM((2 * N, N), BF16),
            pltpu.VMEM((2 * N, 2 * N), BF16),
            pltpu.VMEM((2 * N, 2 * N), BF16),
            pltpu.VMEM((3 * N, 2 * N), BF16),
        ],
        compiler_params=pltpu.CompilerParams(vmem_limit_bytes=limit),
        name="combine",
    )(got, ex, ey, velocity.reshape(3, 2, half, N, N), inv_x, inv_y, wx, wy)
    return out.reshape(velocity.shape)


def solution(mesh):
    return jax.shard_map(
        functools.partial(local, mesh.shape["gx"], mesh.shape["gy"]),
        mesh=mesh,
        in_specs=(
            P(None, None, "gx", "gy"),
            P("gx", None),
            P("gy", None),
            P("gx", None),
            P("gy", None),
            P(None, ("gx", "gy")),
            P(("gx", "gy"), None),
            P(("gx", "gy"), None),
            P(("gx", "gy")),
        ),
        out_specs=P(None, None, "gx", "gy"),
        check_vma=False,
    )
```

```python
import functools

import jax
import jax.numpy as jnp
from jax import lax
from jax.experimental import pallas as pl
from jax.experimental.pallas import tpu as pltpu
from jax.sharding import PartitionSpec as P

HIGH = lax.Precision.HIGHEST
MESH = pl.DeviceIdType.MESH
F32, BF16 = jnp.float32, jnp.bfloat16
N = 128
CAP = 128
BLOCK = CAP + 16
NEAR, FAR = 7.0 / 9.0, 1.0 / 36.0


def iota(shape, dim):
    return lax.broadcasted_iota(jnp.int32, shape, dim)


def mm(a, b):
    return jnp.dot(a, b, preferred_element_type=F32)


def mm_nt(a, b, precision=None):
    return lax.dot_general(a, b, (((1,), (1,)), ((), ())), precision=precision, preferred_element_type=F32)


def split(a):
    hi = a.astype(BF16)
    return hi, (a - hi.astype(F32)).astype(BF16)


def inner_stencil(cell, row):
    gap = cell - row
    return jnp.where(gap == 1, NEAR, 0.0) - jnp.where(gap == -1, NEAR, 0.0) + jnp.where(gap == 2, FAR, 0.0) - jnp.where(gap == -2, FAR, 0.0)


def outer_stencil(row, column, first):
    which = column - first
    low2 = jnp.where((which == 0) & (row == 0), -FAR, 0.0)
    low1 = jnp.where((which == 1) & (row == 0), -NEAR, 0.0) + jnp.where((which == 1) & (row == 1), -FAR, 0.0)
    high1 = jnp.where((which == 2) & (row == N - 1), NEAR, 0.0) + jnp.where((which == 2) & (row == N - 2), FAR, 0.0)
    high2 = jnp.where((which == 3) & (row == N - 1), FAR, 0.0)
    return low2 + low1 + high1 + high2


def last_rows(inverse, spike_t):
    sub, lane = iota((N, N), 0), iota((N, N), 1)
    inner_t = inner_stencil(sub, lane)
    spread = [
        mm_nt(inner_t, jnp.broadcast_to(inverse[N - 2 + a : N - 1 + a, :], (N, N)), HIGH) for a in range(2)
    ]
    outer = jnp.dot(inverse[N - 8 :, :], outer_stencil(sub, lane, 0), precision=HIGH, preferred_element_type=F32)
    part, column = iota((2, N), 0), iota((2, N), 1)
    place = iota((1, N), 1)
    rows = []
    for a in range(2):
        row = outer[6 + a : 7 + a, :]
        for b in range(2):
            picked = jnp.where((part == b) & (column == N - 2 + a), spike_t, 0.0)
            value = jnp.sum(jnp.sum(picked, axis=1, keepdims=True), axis=0, keepdims=True)
            row = row + jnp.where(place == 4 + b, value, 0.0)
        rows.append(row)
    return spread, rows


def chain_y(count, got, reply):
    zero = jnp.zeros(got.shape[1:3] + (1, N), F32)

    def one(d, carry):
        s0, s1, low2, low1 = carry
        here = got[d]
        after = got[jnp.minimum(d + 1, count - 1)]
        more = (d + 1 < count).astype(F32)
        high1, high2 = after[:, :, 2:3, :] * more, after[:, :, 3:4, :] * more
        reply[d] = jnp.concatenate([s0, s1, low2, low1, high1, high2, zero, zero], axis=2)
        new = []
        for a in range(2):
            weight = here[:, :, 6 + a : 7 + a, :]
            total = here[:, :, a : a + 1, :]
            for k, value in enumerate((low2, low1, high1, high2, s0, s1)):
                total = total + weight[:, :, :, k : k + 1] * value
            new.append(total)
        return new[0], new[1], here[:, :, 4:5, :], here[:, :, 5:6, :]

    lax.fori_loop(0, count, one, (zero, zero, zero, zero))


def columns_x(spike_t, inverse):
    sub, lane = iota((N, N), 0), iota((N, N), 1)
    turn = lane % 32
    outer = jnp.dot(inverse, outer_stencil(sub, turn // 4, 2), precision=HIGH, preferred_element_type=F32)
    order = sub % 32 // 4
    spikes = jnp.where(order == 0, spike_t[0:1], jnp.where(order == 1, spike_t[1:2], 0.0)).T
    return outer + spikes


def columns_y(spike_t, inverse):
    sub, lane = iota((N, N), 0), iota((N, N), 1)
    outer = jnp.dot(inverse, outer_stencil(sub, lane % 8, 2), precision=HIGH, preferred_element_type=F32)
    order = sub % 8
    spikes = jnp.where(order == 0, spike_t[0:1], jnp.where(order == 1, spike_t[1:2], 0.0)).T
    return outer + spikes


def inner(inverse):
    sub, lane = iota((N, N), 0), iota((N, N), 1)
    return jnp.dot(inverse, inner_stencil(lane, sub), precision=HIGH, preferred_element_type=F32)


def chain_x(count, got, reply):
    real = iota((1, 4, N), 1) < 3
    zero = jnp.zeros((got.shape[1], 4, N), F32)

    def one(d, carry):
        s0, s1 = carry
        here = got[d]
        reply[d] = jnp.concatenate([s0, s1], axis=1)
        new = []
        for a in range(2):
            weight = here[0:1, 4 * a + 3 : 4 * a + 4, :]
            part = jnp.where(real, here[:, 4 * a : 4 * a + 4, :], 0.0)
            new.append(part + weight[:, :, 4:5] * s0 + weight[:, :, 5:6] * s1)
        return tuple(new)

    lax.fori_loop(0, count, one, (zero, zero))


def whole_kernel(nx, ny, v_hbm, ix_hbm, iy_hbm, wx_hbm, wy_hbm, f_hbm, k_hbm, own_hbm, row_hbm, out_ref,
                 v_ref, ix_ref, iy_ref, wx_ref, wy_ref, f_ref, k_ref, own_ref, row_ref, load_sem,
                 wide_ref, pos_ref, mk_ref, got_mk, qx_ref, my_ref, line_ref,
                 edge_ref, low_ref, high_ref, ex_ref, ey_ref, got_x, got_y, reply_x, reply_y,
                 tile_ref, pick_ref, left_x, left_ex, right_y, right_ey, ext_y,
                 send_m, recv_m, send_x, recv_x, send_y, recv_y,
                 back_send_x, back_recv_x, back_send_y, back_recv_y, edge_send, edge_recv):
    gx, gy = lax.axis_index("gx"), lax.axis_index("gy")
    depth = v_ref.shape[1]
    half = depth // 2
    sx, sy = min(depth, nx), min(depth, ny)
    zx, zy = depth // sx, depth // sy
    chunks = own_ref.shape[0]
    per = 4
    rounds = nx // per
    sub, lane = iota((N, N), 0), iota((N, N), 1)

    pairs = [(own_hbm, own_ref), (row_hbm, row_ref), (f_hbm, f_ref), (k_hbm, k_ref), (v_hbm, v_ref),
             (ix_hbm, ix_ref), (iy_hbm, iy_ref), (wx_hbm, wx_ref), (wy_hbm, wy_ref)]
    loads = [pltpu.make_async_copy(src, dst, load_sem.at[i]) for i, (src, dst) in enumerate(pairs)]
    for load in loads:
        load.start()

    barrier = pltpu.get_barrier_semaphore()

    @pl.loop(1, nx)
    def _(i):
        pl.semaphore_signal(barrier, inc=1, device_id=(lax.rem(gx + i, nx), gy), device_id_type=MESH)

    @pl.loop(1, ny)
    def _(i):
        pl.semaphore_signal(barrier, inc=1, device_id=(gx, lax.rem(gy + i, ny)), device_id_type=MESH)

    def remote(src, dst, send, recv, to):
        return pltpu.make_async_remote_copy(
            src_ref=src, dst_ref=dst, send_sem=send, recv_sem=recv, device_id=to, device_id_type=MESH)

    def out_x(to, origin):
        return remote(qx_ref.at[pl.ds(to * zx, zx)], got_x.at[origin], send_x.at[to], recv_x.at[origin], (to, gy))

    def out_y(to, origin):
        return remote(my_ref.at[pl.ds(to * zy, zy)], got_y.at[origin], send_y.at[to], recv_y.at[origin], (gx, to))

    def out_m(to, origin):
        return remote(mk_ref.at[to], got_mk.at[origin], send_m.at[to], recv_m.at[origin], (to, gy))

    def back_x(to, origin):
        return remote(reply_x.at[to], ex_ref.at[pl.ds(origin * zx, zx)], back_send_x.at[to], back_recv_x.at[origin], (to, gy))

    def back_y(to, origin):
        return remote(reply_y.at[to], ey_ref.at[pl.ds(origin * zy, zy)], back_send_y.at[to], back_recv_y.at[origin], (gx, to))

    def edge_low():
        return remote(edge_ref.at[1], low_ref, edge_send.at[0], edge_recv.at[0], (jnp.minimum(gx + 1, nx - 1), gy))

    def edge_high():
        return remote(edge_ref.at[0], high_ref, edge_send.at[1], edge_recv.at[1], (jnp.maximum(gx - 1, 0), gy))

    for load in loads[:4]:
        load.wait()
    upto = jnp.concatenate([(sub <= lane).astype(BF16), jnp.ones((N, N), BF16)], axis=1)
    name = iota((nx, N), 0)
    before = jnp.zeros((nx, N), F32)
    for k in range(chunks):
        owner = own_ref[k : k + 1, :]
        hit = name == owner
        counted = mm(hit.astype(F32).astype(BF16), upto)
        rank = counted[:, :N] + before - 1.0
        before = before + counted[:, N:]
        place = jnp.sum(jnp.where(hit, rank, 0.0), axis=0, keepdims=True)
        pos_ref[0:1, k * N : (k + 1) * N] = owner.astype(F32)
        pos_ref[1:2, k * N : (k + 1) * N] = place

        cell = row_ref[k : k + 1, :]
        plane = cell // N
        upper = plane >= half
        three = f_ref[:, k * N : (k + 1) * N].astype(F32)
        facts = jnp.concatenate(
            [jnp.where(upper, 0.0, three), jnp.where(upper, three, 0.0),
             (plane % half).astype(F32), (cell % N).astype(F32)],
            axis=0,
        )
        wide_ref[k * N : (k + 1) * N, 0:N] = k_ref[k * N : (k + 1) * N, :]
        wide_ref[k * N : (k + 1) * N, N:] = jnp.tile(facts, (N // 8, 1)).T.astype(BF16)

    for load in loads[4:]:
        load.wait()
    blank = jnp.zeros((depth, 1, N), F32)
    for e, first in enumerate((0, N - 2)):
        edge_ref[e] = jnp.concatenate(
            [p for a in range(2) for p in [v_ref[c, :, first + a : first + a + 1, :] for c in range(3)] + [blank]], axis=1)

    pl.semaphore_wait(barrier, nx + ny - 2)

    @pl.when(gx < nx - 1)
    def _():
        edge_low().start()

    @pl.when(gx > 0)
    def _():
        edge_high().start()

    slot = iota((CAP, 1), 0).astype(F32).astype(BF16)

    def compact(low, high):
        @pl.loop(low, high)
        def _(step):
            owner, place = pos_ref[0:1, :], pos_ref[1:2, :]
            picks = []
            for i in range(per):
                to = lax.rem(gx + step * per + i, nx)
                mine = jnp.where(owner == to.astype(F32), place, -1.0).astype(BF16)
                picks.append(jnp.where(mine == slot, jnp.ones((), BF16), jnp.zeros((), BF16)))
            rows = mm(jnp.concatenate(picks, axis=0), wide_ref[...])
            for i in range(per):
                off = step * per + i
                to = lax.rem(gx + off, nx)
                part = rows[i * CAP : (i + 1) * CAP]
                mk_ref[to, 0:CAP, :] = part[:, :N].astype(BF16)
                facts_t = part[:, N:].T[0:8, :]
                mk_ref[to, CAP:, :] = jnp.concatenate([facts_t, jnp.zeros((8, N), F32)], axis=0).astype(BF16)

                @pl.when(off > 0)
                def _():
                    out_m(to, gx).start()

                @pl.when(off == 0)
                def _():
                    got_mk[gx] = mk_ref[gx]

    cuts = (0, rounds // 4, 5 * rounds // 8, rounds)
    compact(cuts[0], cuts[1])

    (sy0, sy1), (cy0, cy1) = last_rows(iy_ref[...], wy_ref[...])
    kind = lane % 8
    base = jnp.where(kind == 0, sy0, jnp.where(kind == 1, sy1, 0.0))
    for i, cell in enumerate((0, 1, N - 2, N - 1)):
        base = base + jnp.where((kind == 2 + i) & (sub == cell), 1.0, 0.0)
    base_hi, base_lo = (p.astype(F32) for p in split(base))
    line_ref[...] = jnp.zeros_like(line_ref)

    @pl.loop(0, depth)
    def _(z):
        mine = lane // 8 == z
        hi = jnp.where(mine, base_hi, 0.0).astype(BF16)
        lo = jnp.where(mine, base_lo, 0.0).astype(BF16)
        v_hi, v_lo = split(v_ref[:, z].reshape(3 * N, N))
        line_ref[...] += mm(jnp.concatenate([v_hi, v_lo], axis=1), jnp.concatenate([hi, hi], axis=0)) + mm(v_hi, lo)

    kind_row = sub % 8
    for c in range(3):
        lines = line_ref[c * N : (c + 1) * N, :].T
        lines = jnp.where(kind_row == 6, cy0, jnp.where(kind_row == 7, cy1, lines))
        my_ref[:, c] = lines.reshape(depth, 8, N)

    @pl.loop(1, ny)
    def _(i):
        out_y(lax.rem(gy + i, ny), gy).start()

    (sx0, sx1), (cx0, cx1) = last_rows(ix_ref[...], wx_ref[...])

    @pl.loop(0, depth)
    def _(z):
        rows = []
        for weight, known in ((sx0, cx0), (sx1, cx1)):
            rows += [jnp.sum(v_ref[c, z] * weight, axis=0, keepdims=True) for c in range(3)] + [known]
        qx_ref[z] = jnp.concatenate(rows, axis=0)

    @pl.when(gx == 0)
    def _():
        low_ref[...] = jnp.zeros_like(low_ref)

    @pl.when(gx == nx - 1)
    def _():
        high_ref[...] = jnp.zeros_like(high_ref)

    @pl.when(gx > 0)
    def _():
        edge_low().wait_recv()

    @pl.when(gx < nx - 1)
    def _():
        edge_high().wait_recv()

    outer = [low_ref[:, 0:4], low_ref[:, 4:8], high_ref[:, 0:4], high_ref[:, 4:8]]
    for a, known in ((0, cx0), (1, cx1)):
        total = qx_ref[:, 4 * a : 4 * a + 4]
        for k in range(4):
            total = total + known[:, k : k + 1].reshape(1, 1, 1) * outer[k]
        qx_ref[:, 4 * a : 4 * a + 4] = total

    @pl.loop(0, sx)
    def _(i):
        to = lax.rem(gx + i, sx)

        @pl.when(to != gx)
        def _():
            out_x(to, gx).start()

    compact(cuts[1], cuts[2])

    got_y[gy] = my_ref[pl.ds(gy * zy, zy)]

    @pl.loop(1, ny)
    def _(i):
        out_y(gy, lax.rem(gy + i, ny)).wait_recv()

    chain_y(ny, got_y, reply_y)

    @pl.loop(1, ny)
    def _(i):
        back_y(lax.rem(gy + i, ny), gy).start()

    ey_ref[pl.ds(gy * zy, zy)] = reply_y[gy]

    @pl.when(gx < sx)
    def _():
        got_x[gx] = qx_ref[pl.ds(gx * zx, zx)]

        @pl.loop(1, nx)
        def _(i):
            out_x(gx, lax.rem(gx + i, nx)).wait_recv()

        chain_x(nx, got_x, reply_x)

        @pl.loop(1, nx)
        def _(i):
            back_x(lax.rem(gx + i, nx), gx).start()

        ex_ref[pl.ds(gx * zx, zx)] = reply_x[gx]

    compact(cuts[2], cuts[3])

    out_ref[...] = jnp.zeros_like(out_ref)
    hi, lo = split(inner(ix_ref[...]))
    left_x[0:N, 0:N], left_x[0:N, N:] = hi, hi
    left_x[N:, 0:N], left_x[N:, N:] = lo, lo
    cols = columns_x(wx_ref[...], ix_ref[...])
    for c in range(3):
        hi, lo = split(jnp.where(lane % 4 == c, cols, 0.0))
        left_ex[2 * c * N : (2 * c + 1) * N], left_ex[(2 * c + 1) * N : (2 * c + 2) * N] = hi, lo
    hi, lo = split(inner(iy_ref[...]).T)
    right_y[0:N, 0:N], right_y[0:N, N:] = hi, lo
    right_y[N:, 0:N], right_y[N:, N:] = hi, lo
    hi, lo = split(columns_y(wy_ref[...], iy_ref[...]).T)
    right_ey[0:N, 0:N], right_ey[0:N, N:] = hi, lo
    right_ey[N:, 0:N], right_ey[N:, N:] = hi, lo

    def scatter(low, high):
        @pl.loop(low, high)
        def _(step):
            facts = []
            for i in range(per):
                off = step * per + i
                source = lax.rem(gx + nx - off, nx)

                @pl.when(off > 0)
                def _():
                    out_m(gx, source).wait_recv()

                facts.append(got_mk[source, CAP:, :].astype(F32)[0:8])
            stack = jnp.concatenate(facts, axis=0)
            columns = jnp.tile(stack, (N // (8 * per), 1)).T
            for i in range(per):
                source = lax.rem(gx + nx - (step * per + i), nx)
                rows = got_mk[source, 0:CAP, :].astype(F32)
                for k in range(6):
                    tile_ref[i * CAP : (i + 1) * CAP, k * N : (k + 1) * N] = (rows * columns[:, 8 * i + k : 8 * i + k + 1]).astype(BF16)
                for zz in range(half):
                    mine = jnp.where(facts[i][6:7] == float(zz), facts[i][7:8], -1.0).astype(BF16)
                    pick_ref[zz * N : (zz + 1) * N, i * CAP : (i + 1) * CAP] = jnp.where(
                        mine == slot, jnp.ones((), BF16), jnp.zeros((), BF16))
            for h in range(2):
                for r in range(2):
                    count = half // 2
                    more = mm(pick_ref[r * count * N : (r + 1) * count * N, :], tile_ref[:, h * 3 * N : (h + 1) * 3 * N])
                    for c in range(3):
                        at = slice(h * half + r * count, h * half + (r + 1) * count)
                        out_ref[c, at] += 0.5 * more[:, c * N : (c + 1) * N].reshape(count, N, N)

    scatter(0, cuts[2])

    @pl.loop(1, ny)
    def _(i):
        back_y(gy, lax.rem(gy + i, ny)).wait_recv()

    @pl.loop(0, sx)
    def _(i):
        other = lax.rem(gx + i, sx)

        @pl.when(other != gx)
        def _():
            back_x(gx, other).wait_recv()

    for c in range(3):
        hi, lo = split(ey_ref[:, c].reshape(8 * depth, N).T)
        ext_y[c * N : (c + 1) * N, 0:N], ext_y[c * N : (c + 1) * N, N:] = hi, lo

    @pl.loop(0, half)
    def _(step):
        zs = [step, step + half]
        vs = [[v_ref[c, z] for c in range(3)] for z in zs]
        parts = [[split(v) for v in line] for line in vs]
        wide = jnp.concatenate([jnp.concatenate([hi, lo], axis=0) for line in parts for hi, lo in line], axis=1)
        both = mm(left_x[...], wide)
        ends = []
        for z in zs:
            hi, lo = split(jnp.concatenate([ex_ref[z], low_ref[z], high_ref[z], jnp.zeros((8, N), F32)], axis=0))
            ends.append(jnp.concatenate([hi, lo], axis=0))
        bent = mm(left_ex[:, 0:64], jnp.concatenate(ends, axis=1))
        for h, z in enumerate(zs):
            tall = jnp.concatenate([jnp.concatenate([hi, lo], axis=1) for hi, lo in parts[h]], axis=0)
            mine = iota((2 * N, 2 * N), 0) % N // 8 == z
            right_ext = jnp.where(mine, right_ey[...].astype(F32), 0.0).astype(BF16)
            across = mm(tall, right_y[...]) + mm(ext_y[...], right_ext)
            for c in range(3):
                k = h * 3 + c
                dx = both[:N, k * N : (k + 1) * N] + both[N:, k * N : (k + 1) * N]
                dx = dx + bent[2 * c * N : (2 * c + 1) * N, h * N : (h + 1) * N] + bent[(2 * c + 1) * N : (2 * c + 2) * N, h * N : (h + 1) * N]
                dy = across[c * N : (c + 1) * N, :N] + across[c * N : (c + 1) * N, N:]
                out_ref[c, z] += vs[h][c] - 0.5 * (vs[h][0] * dx + vs[h][1] * dy)

    scatter(cuts[2], cuts[3])

    @pl.loop(1, ny)
    def _(i):
        other = lax.rem(gy + i, ny)
        out_y(other, gy).wait_send()
        back_y(other, gy).wait_send()

    @pl.loop(0, sx)
    def _(i):
        other = lax.rem(gx + i, sx)

        @pl.when(other != gx)
        def _():
            out_x(other, gx).wait_send()

    @pl.when(gx < sx)
    def _():
        @pl.loop(1, nx)
        def _(i):
            back_x(lax.rem(gx + i, nx), gx).wait_send()

    @pl.loop(1, nx)
    def _(i):
        out_m(lax.rem(gx + i, nx), gx).wait_send()

    @pl.when(gx < nx - 1)
    def _():
        edge_low().wait_send()

    @pl.when(gx > 0)
    def _():
        edge_high().wait_send()


def local(nx, ny, velocity, inv_x, inv_y, spike_x, spike_y, marker_force, marker_kernel, marker_owner, marker_row):
    depth = velocity.shape[1]
    half = depth // 2
    slots = marker_row.shape[0]
    args = (velocity, inv_x, inv_y, spike_x.T, spike_y.T, marker_force, marker_kernel,
            marker_owner.reshape(slots // N, N), marker_row.reshape(slots // N, N))
    sx, sy = min(depth, nx), min(depth, ny)
    dma, vmem = pltpu.SemaphoreType.DMA, pltpu.VMEM
    return pl.pallas_call(
        functools.partial(whole_kernel, nx, ny),
        out_shape=jax.ShapeDtypeStruct(velocity.shape, F32),
        in_specs=[pl.BlockSpec(memory_space=pl.ANY)] * len(args),
        out_specs=pl.BlockSpec(memory_space=pltpu.VMEM),
        scratch_shapes=[vmem(a.shape, a.dtype) for a in args] + [
            dma((len(args),)),
            vmem((slots, 2 * N), BF16),
            vmem((8, slots), F32),
            vmem((nx, BLOCK, N), BF16),
            vmem((nx, BLOCK, N), BF16),
            vmem((depth, 8, N), F32),
            vmem((depth, 3, 8, N), F32),
            vmem((3 * N, N), F32),
            vmem((2, depth, 8, N), F32),
            vmem((depth, 8, N), F32),
            vmem((depth, 8, N), F32),
            vmem((depth, 8, N), F32),
            vmem((depth, 3, 8, N), F32),
            vmem((nx, depth // sx, 8, N), F32),
            vmem((ny, depth // sy, 3, 8, N), F32),
            vmem((nx, depth // sx, 8, N), F32),
            vmem((ny, depth // sy, 3, 8, N), F32),
            vmem((4 * CAP, 6 * N), BF16),
            vmem((half * N, 4 * CAP), BF16),
            vmem((2 * N, 2 * N), BF16),
            vmem((6 * N, N), BF16),
            vmem((2 * N, 2 * N), BF16),
            vmem((2 * N, 2 * N), BF16),
            vmem((3 * N, 2 * N), BF16),
            dma((nx,)), dma((nx,)), dma((sx,)), dma((nx,)), dma((ny,)), dma((ny,)),
            dma((nx,)), dma((sx,)), dma((ny,)), dma((ny,)), dma((2,)), dma((2,)),
        ],
        compiler_params=pltpu.CompilerParams(vmem_limit_bytes=56 * 1024 * 1024, collective_id=0, has_side_effects=True),
        name="section",
    )(*args)


def solution(mesh):
    return jax.shard_map(
        functools.partial(local, mesh.shape["gx"], mesh.shape["gy"]),
        mesh=mesh,
        in_specs=(
            P(None, None, "gx", "gy"),
            P("gx", None),
            P("gy", None),
            P("gx", None),
            P("gy", None),
            P(None, ("gx", "gy")),
            P(("gx", "gy"), None),
            P(("gx", "gy"), None),
            P(("gx", "gy")),
        ),
        out_specs=P(None, None, "gx", "gy"),
        check_vma=False,
    )
```

```python
import functools

import jax
import jax.numpy as jnp
from jax import lax
from jax.experimental import pallas as pl
from jax.experimental.pallas import tpu as pltpu
from jax.sharding import PartitionSpec as P

HIGH = lax.Precision.HIGHEST
MESH = pl.DeviceIdType.MESH
F32, BF16 = jnp.float32, jnp.bfloat16
N = 128
CAP = 128
BLOCK = CAP + 16
NEAR, FAR = 7.0 / 9.0, 1.0 / 36.0


def iota(shape, dim):
    return lax.broadcasted_iota(jnp.int32, shape, dim)


def mm(a, b):
    return jnp.dot(a, b, preferred_element_type=F32)


def mm_nt(a, b, precision=None):
    return lax.dot_general(a, b, (((1,), (1,)), ((), ())), precision=precision, preferred_element_type=F32)


def split(a):
    hi = a.astype(BF16)
    return hi, (a - hi.astype(F32)).astype(BF16)


def inner_stencil(cell, row):
    gap = cell - row
    return jnp.where(gap == 1, NEAR, 0.0) - jnp.where(gap == -1, NEAR, 0.0) + jnp.where(gap == 2, FAR, 0.0) - jnp.where(gap == -2, FAR, 0.0)


def outer_stencil(row, column, first):
    which = column - first
    low2 = jnp.where((which == 0) & (row == 0), -FAR, 0.0)
    low1 = jnp.where((which == 1) & (row == 0), -NEAR, 0.0) + jnp.where((which == 1) & (row == 1), -FAR, 0.0)
    high1 = jnp.where((which == 2) & (row == N - 1), NEAR, 0.0) + jnp.where((which == 2) & (row == N - 2), FAR, 0.0)
    high2 = jnp.where((which == 3) & (row == N - 1), FAR, 0.0)
    return low2 + low1 + high1 + high2


def last_rows(inverse, spike_t):
    sub, lane = iota((N, N), 0), iota((N, N), 1)
    inner_t = inner_stencil(sub, lane)
    spread = [
        mm_nt(inner_t, jnp.broadcast_to(inverse[N - 2 + a : N - 1 + a, :], (N, N)), HIGH) for a in range(2)
    ]
    outer = jnp.dot(inverse[N - 8 :, :], outer_stencil(sub, lane, 0), precision=HIGH, preferred_element_type=F32)
    part, column = iota((2, N), 0), iota((2, N), 1)
    place = iota((1, N), 1)
    rows = []
    for a in range(2):
        row = outer[6 + a : 7 + a, :]
        for b in range(2):
            picked = jnp.where((part == b) & (column == N - 2 + a), spike_t, 0.0)
            value = jnp.sum(jnp.sum(picked, axis=1, keepdims=True), axis=0, keepdims=True)
            row = row + jnp.where(place == 4 + b, value, 0.0)
        rows.append(row)
    return spread, rows


def chain_y(count, got, reply):
    zero = jnp.zeros(got.shape[1:3] + (1, N), F32)

    def one(d, carry):
        s0, s1, low2, low1 = carry
        here = got[d]
        after = got[jnp.minimum(d + 1, count - 1)]
        more = (d + 1 < count).astype(F32)
        high1, high2 = after[:, :, 2:3, :] * more, after[:, :, 3:4, :] * more
        reply[d] = jnp.concatenate([s0, s1, low2, low1, high1, high2, zero, zero], axis=2)
        new = []
        for a in range(2):
            weight = here[:, :, 6 + a : 7 + a, :]
            total = here[:, :, a : a + 1, :]
            for k, value in enumerate((low2, low1, high1, high2, s0, s1)):
                total = total + weight[:, :, :, k : k + 1] * value
            new.append(total)
        return new[0], new[1], here[:, :, 4:5, :], here[:, :, 5:6, :]

    lax.fori_loop(0, count, one, (zero, zero, zero, zero), unroll=2)


def columns_x(spike_t, inverse):
    sub, lane = iota((N, N), 0), iota((N, N), 1)
    turn = lane % 32
    outer = jnp.dot(inverse, outer_stencil(sub, turn // 4, 2), precision=HIGH, preferred_element_type=F32)
    order = sub % 32 // 4
    spikes = jnp.where(order == 0, spike_t[0:1], jnp.where(order == 1, spike_t[1:2], 0.0)).T
    return outer + spikes


def columns_y(spike_t, inverse):
    sub, lane = iota((N, N), 0), iota((N, N), 1)
    outer = jnp.dot(inverse, outer_stencil(sub, lane % 8, 2), precision=HIGH, preferred_element_type=F32)
    order = sub % 8
    spikes = jnp.where(order == 0, spike_t[0:1], jnp.where(order == 1, spike_t[1:2], 0.0)).T
    return outer + spikes


def inner(inverse):
    sub, lane = iota((N, N), 0), iota((N, N), 1)
    return jnp.dot(inverse, inner_stencil(lane, sub), precision=HIGH, preferred_element_type=F32)


def chain_x(count, got, reply):
    real = iota((1, 4, N), 1) < 3
    zero = jnp.zeros((got.shape[1], 4, N), F32)

    def one(d, carry):
        s0, s1 = carry
        here = got[d]
        reply[d] = jnp.concatenate([s0, s1], axis=1)
        new = []
        for a in range(2):
            weight = here[0:1, 4 * a + 3 : 4 * a + 4, :]
            part = jnp.where(real, here[:, 4 * a : 4 * a + 4, :], 0.0)
            new.append(part + weight[:, :, 4:5] * s0 + weight[:, :, 5:6] * s1)
        return tuple(new)

    lax.fori_loop(0, count, one, (zero, zero), unroll=min(count, 8))


def whole_kernel(nx, ny, v_hbm, ix_hbm, iy_hbm, wx_hbm, wy_hbm, f_hbm, k_hbm, own_hbm, row_hbm, out_hbm,
                 v_ref, ix_ref, iy_ref, wx_ref, wy_ref, f_ref, k_ref, own_ref, row_ref, load_sem,
                 wide_ref, pos_ref, mk_ref, got_mk, qx_ref, my_ref, line_ref,
                 edge_ref, low_ref, high_ref, ex_ref, ey_ref, got_x, got_y, reply_x, reply_y,
                 tile_ref, pick_ref, left_x, left_ex, right_y, right_ey, ext_y,
                 send_m, recv_m, send_x, recv_x, send_y, recv_y,
                 back_send_x, back_recv_x, back_send_y, back_recv_y, edge_send, edge_recv, out_ref, store_sem):
    gx, gy = lax.axis_index("gx"), lax.axis_index("gy")
    depth = v_ref.shape[1]
    half = depth // 2
    sx, sy = min(depth, nx), min(depth, ny)
    zx, zy = depth // sx, depth // sy
    chunks = own_ref.shape[0]
    per = 4
    rounds = nx // per
    sub, lane = iota((N, N), 0), iota((N, N), 1)

    pairs = [(own_hbm, own_ref), (row_hbm, row_ref), (f_hbm, f_ref), (k_hbm, k_ref), (v_hbm, v_ref),
             (ix_hbm, ix_ref), (iy_hbm, iy_ref), (wx_hbm, wx_ref), (wy_hbm, wy_ref)]
    loads = [pltpu.make_async_copy(src, dst, load_sem.at[i]) for i, (src, dst) in enumerate(pairs)]
    for load in loads:
        load.start()

    barrier = pltpu.get_barrier_semaphore()

    @pl.loop(1, nx)
    def _(i):
        pl.semaphore_signal(barrier, inc=1, device_id=(lax.rem(gx + i, nx), gy), device_id_type=MESH)

    @pl.loop(1, ny)
    def _(i):
        pl.semaphore_signal(barrier, inc=1, device_id=(gx, lax.rem(gy + i, ny)), device_id_type=MESH)

    def remote(src, dst, send, recv, to):
        return pltpu.make_async_remote_copy(
            src_ref=src, dst_ref=dst, send_sem=send, recv_sem=recv, device_id=to, device_id_type=MESH)

    def out_x(to, origin):
        return remote(qx_ref.at[pl.ds(to * zx, zx)], got_x.at[origin], send_x.at[to], recv_x.at[origin], (to, gy))

    def out_y(to, origin):
        return remote(my_ref.at[pl.ds(to * zy, zy)], got_y.at[origin], send_y.at[to], recv_y.at[origin], (gx, to))

    def out_m(to, origin):
        return remote(mk_ref.at[to], got_mk.at[origin], send_m.at[to], recv_m.at[origin], (to, gy))

    def back_x(to, origin):
        return remote(reply_x.at[to], ex_ref.at[pl.ds(origin * zx, zx)], back_send_x.at[to], back_recv_x.at[origin], (to, gy))

    def back_y(to, origin):
        return remote(reply_y.at[to], ey_ref.at[pl.ds(origin * zy, zy)], back_send_y.at[to], back_recv_y.at[origin], (gx, to))

    def edge_low():
        return remote(edge_ref.at[1], low_ref, edge_send.at[0], edge_recv.at[0], (jnp.minimum(gx + 1, nx - 1), gy))

    def edge_high():
        return remote(edge_ref.at[0], high_ref, edge_send.at[1], edge_recv.at[1], (jnp.maximum(gx - 1, 0), gy))

    for load in loads[:4]:
        load.wait()
    upto = jnp.concatenate([(sub <= lane).astype(BF16), jnp.ones((N, N), BF16)], axis=1)
    name = iota((nx, N), 0)
    before = jnp.zeros((nx, N), F32)
    for k in range(chunks):
        owner = own_ref[k : k + 1, :]
        hit = name == owner
        counted = mm(hit.astype(F32).astype(BF16), upto)
        rank = counted[:, :N] + before - 1.0
        before = before + counted[:, N:]
        place = jnp.sum(jnp.where(hit, rank, 0.0), axis=0, keepdims=True)
        pos_ref[0:1, k * N : (k + 1) * N] = owner.astype(F32)
        pos_ref[1:2, k * N : (k + 1) * N] = place

        cell = row_ref[k : k + 1, :]
        plane = cell // N
        upper = plane >= half
        three = f_ref[:, k * N : (k + 1) * N].astype(F32)
        facts = jnp.concatenate(
            [jnp.where(upper, 0.0, three), jnp.where(upper, three, 0.0),
             (plane % half).astype(F32), (cell % N).astype(F32)],
            axis=0,
        )
        wide_ref[k * N : (k + 1) * N, 0:N] = k_ref[k * N : (k + 1) * N, :]
        wide_ref[k * N : (k + 1) * N, N:] = jnp.tile(facts, (N // 8, 1)).T.astype(BF16)

    for load in loads[4:]:
        load.wait()
    blank = jnp.zeros((depth, 1, N), F32)
    for e, first in enumerate((0, N - 2)):
        edge_ref[e] = jnp.concatenate(
            [p for a in range(2) for p in [v_ref[c, :, first + a : first + a + 1, :] for c in range(3)] + [blank]], axis=1)

    pl.semaphore_wait(barrier, nx + ny - 2)

    @pl.when(gx < nx - 1)
    def _():
        edge_low().start()

    @pl.when(gx > 0)
    def _():
        edge_high().start()

    slot = iota((CAP, 1), 0).astype(F32).astype(BF16)

    def compact(low, high):
        @pl.loop(low, high)
        def _(step):
            owner, place = pos_ref[0:1, :], pos_ref[1:2, :]
            picks = []
            for i in range(per):
                to = lax.rem(gx + step * per + i, nx)
                mine = jnp.where(owner == to.astype(F32), place, -1.0).astype(BF16)
                picks.append(jnp.where(mine == slot, jnp.ones((), BF16), jnp.zeros((), BF16)))
            rows = mm(jnp.concatenate(picks, axis=0), wide_ref[...])
            for i in range(per):
                off = step * per + i
                to = lax.rem(gx + off, nx)
                part = rows[i * CAP : (i + 1) * CAP]
                mk_ref[to, 0:CAP, :] = part[:, :N].astype(BF16)
                facts_t = part[:, N:].T[0:8, :]
                mk_ref[to, CAP:, :] = jnp.concatenate([facts_t, jnp.zeros((8, N), F32)], axis=0).astype(BF16)

                @pl.when(off > 0)
                def _():
                    out_m(to, gx).start()

                @pl.when(off == 0)
                def _():
                    got_mk[gx] = mk_ref[gx]

    cuts = (0, max(1, rounds // 4), max(1, 3 * rounds // 4), rounds)
    compact(cuts[0], cuts[1])

    (sy0, sy1), (cy0, cy1) = last_rows(iy_ref[...], wy_ref[...])
    kind = lane % 8
    base = jnp.where(kind == 0, sy0, jnp.where(kind == 1, sy1, 0.0))
    for i, cell in enumerate((0, 1, N - 2, N - 1)):
        base = base + jnp.where((kind == 2 + i) & (sub == cell), 1.0, 0.0)
    base_hi, base_lo = (p.astype(F32) for p in split(base))
    line_ref[...] = jnp.zeros_like(line_ref)

    @pl.loop(0, depth)
    def _(z):
        mine = lane // 8 == z
        hi = jnp.where(mine, base_hi, 0.0).astype(BF16)
        lo = jnp.where(mine, base_lo, 0.0).astype(BF16)
        v_hi, v_lo = split(v_ref[:, z].reshape(3 * N, N))
        line_ref[...] += mm(jnp.concatenate([v_hi, v_lo], axis=1), jnp.concatenate([hi, hi], axis=0)) + mm(v_hi, lo)

    kind_row = sub % 8
    for c in range(3):
        lines = line_ref[c * N : (c + 1) * N, :].T
        lines = jnp.where(kind_row == 6, cy0, jnp.where(kind_row == 7, cy1, lines))
        my_ref[:, c] = lines.reshape(depth, 8, N)

    @pl.loop(1, ny)
    def _(i):
        out_y(lax.rem(gy + i, ny), gy).start()

    (sx0, sx1), (cx0, cx1) = last_rows(ix_ref[...], wx_ref[...])

    @pl.loop(0, depth)
    def _(z):
        rows = []
        for weight, known in ((sx0, cx0), (sx1, cx1)):
            rows += [jnp.sum(v_ref[c, z] * weight, axis=0, keepdims=True) for c in range(3)] + [known]
        qx_ref[z] = jnp.concatenate(rows, axis=0)

    @pl.when(gx == 0)
    def _():
        low_ref[...] = jnp.zeros_like(low_ref)

    @pl.when(gx == nx - 1)
    def _():
        high_ref[...] = jnp.zeros_like(high_ref)

    @pl.when(gx > 0)
    def _():
        edge_low().wait_recv()

    @pl.when(gx < nx - 1)
    def _():
        edge_high().wait_recv()

    outer = [low_ref[:, 0:4], low_ref[:, 4:8], high_ref[:, 0:4], high_ref[:, 4:8]]
    for a, known in ((0, cx0), (1, cx1)):
        total = qx_ref[:, 4 * a : 4 * a + 4]
        for k in range(4):
            total = total + known[:, k : k + 1].reshape(1, 1, 1) * outer[k]
        qx_ref[:, 4 * a : 4 * a + 4] = total

    @pl.loop(0, sx)
    def _(i):
        to = lax.rem(gx + i, sx)

        @pl.when(to != gx)
        def _():
            out_x(to, gx).start()

    compact(cuts[1], cuts[2])

    many = nx // 4
    choice = jnp.full((), 0.5, BF16)
    out_ref[...] = jnp.zeros_like(out_ref)

    def stores(h, r):
        count = half // 2
        at = pl.ds(h * half + r * count, count)
        return [pltpu.make_async_copy(out_ref.at[c, at], out_hbm.at[c, at], store_sem.at[6 * h + 3 * r + c]) for c in range(3)]

    def scatter_one(step, last):
        facts = []
        for i in range(many):
            off = step * many + i
            source = lax.rem(gx + nx - off, nx)

            @pl.when(off > 0)
            def _():
                out_m(gx, source).wait_recv()

            facts.append(got_mk[source, CAP:, :].astype(F32)[0:8])
        stack = jnp.concatenate(facts, axis=0)
        columns = jnp.tile(stack, (N // (8 * many), 1)).T.astype(BF16)
        for i in range(many):
            source = lax.rem(gx + nx - (step * many + i), nx)
            rows = got_mk[source, 0:CAP, :]
            for k in range(6):
                tile_ref[i * CAP : (i + 1) * CAP, k * N : (k + 1) * N] = rows * columns[:, 8 * i + k : 8 * i + k + 1]
            for zz in range(half):
                mine = jnp.where(facts[i][6:7] == float(zz), facts[i][7:8], -1.0).astype(BF16)
                pick_ref[zz * N : (zz + 1) * N, i * CAP : (i + 1) * CAP] = jnp.where(mine == slot, choice, jnp.zeros((), BF16))
        for h in range(2):
            for r in range(2):
                count = half // 2
                more = mm(pick_ref[r * count * N : (r + 1) * count * N, :], tile_ref[:, h * 3 * N : (h + 1) * 3 * N])
                for c in range(3):
                    at = slice(h * half + r * count, h * half + (r + 1) * count)
                    out_ref[c, at] += more[:, c * N : (c + 1) * N].reshape(count, N, N)
                if last:
                    for store in stores(h, r):
                        store.start()

    def scatter(low, high):
        @pl.loop(low, high)
        def _(step):
            scatter_one(step, False)

    hi, lo = split(inner(ix_ref[...]))
    left_x[0:N, 0:N], left_x[0:N, N:] = hi, hi
    left_x[N:, 0:N], left_x[N:, N:] = lo, lo
    cols = columns_x(wx_ref[...], ix_ref[...])
    for c in range(3):
        hi, lo = split(jnp.where(lane % 4 == c, cols, 0.0))
        left_ex[2 * c * N : (2 * c + 1) * N], left_ex[(2 * c + 1) * N : (2 * c + 2) * N] = hi, lo
    hi, lo = split(inner(iy_ref[...]).T)
    right_y[0:N, 0:N], right_y[0:N, N:] = hi, lo
    right_y[N:, 0:N], right_y[N:, N:] = hi, lo
    hi, lo = split(columns_y(wy_ref[...], iy_ref[...]).T)
    right_ey[0:N, 0:N], right_ey[0:N, N:] = hi, lo
    right_ey[N:, 0:N], right_ey[N:, N:] = hi, lo

    scatter(0, 1)

    got_y[gy] = my_ref[pl.ds(gy * zy, zy)]

    @pl.loop(1, ny)
    def _(i):
        out_y(gy, lax.rem(gy + i, ny)).wait_recv()

    chain_y(ny, got_y, reply_y)

    @pl.loop(1, ny)
    def _(i):
        back_y(lax.rem(gy + i, ny), gy).start()

    ey_ref[pl.ds(gy * zy, zy)] = reply_y[gy]

    @pl.when(gx < sx)
    def _():
        got_x[gx] = qx_ref[pl.ds(gx * zx, zx)]

        @pl.loop(1, nx)
        def _(i):
            out_x(gx, lax.rem(gx + i, nx)).wait_recv()

        chain_x(nx, got_x, reply_x)

        @pl.loop(1, nx)
        def _(i):
            back_x(lax.rem(gx + i, nx), gx).start()

        ex_ref[pl.ds(gx * zx, zx)] = reply_x[gx]

    compact(cuts[2], cuts[3])

    scatter(1, nx // many - 1)

    @pl.loop(1, ny)
    def _(i):
        back_y(gy, lax.rem(gy + i, ny)).wait_recv()

    @pl.loop(0, sx)
    def _(i):
        other = lax.rem(gx + i, sx)

        @pl.when(other != gx)
        def _():
            back_x(gx, other).wait_recv()

    for c in range(3):
        hi, lo = split(ey_ref[:, c].reshape(8 * depth, N).T)
        ext_y[c * N : (c + 1) * N, 0:N], ext_y[c * N : (c + 1) * N, N:] = hi, lo

    @pl.loop(0, half)
    def _(step):
        zs = [step, step + half]
        vs = [[v_ref[c, z] for c in range(3)] for z in zs]
        parts = [[split(v) for v in line] for line in vs]
        wide = jnp.concatenate([jnp.concatenate([hi, lo], axis=0) for line in parts for hi, lo in line], axis=1)
        both = mm(left_x[...], wide)
        ends = []
        for z in zs:
            hi, lo = split(jnp.concatenate([ex_ref[z], low_ref[z], high_ref[z], jnp.zeros((8, N), F32)], axis=0))
            ends.append(jnp.concatenate([hi, lo], axis=0))
        bent = mm(left_ex[:, 0:64], jnp.concatenate(ends, axis=1))
        for h, z in enumerate(zs):
            tall = jnp.concatenate([jnp.concatenate([hi, lo], axis=1) for hi, lo in parts[h]], axis=0)
            mine = iota((2 * N, 2 * N), 0) % N // 8 == z
            right_ext = jnp.where(mine, right_ey[...].astype(F32), 0.0).astype(BF16)
            across = mm(tall, right_y[...]) + mm(ext_y[...], right_ext)
            for c in range(3):
                k = h * 3 + c
                dx = both[:N, k * N : (k + 1) * N] + both[N:, k * N : (k + 1) * N]
                dx = dx + bent[2 * c * N : (2 * c + 1) * N, h * N : (h + 1) * N] + bent[(2 * c + 1) * N : (2 * c + 2) * N, h * N : (h + 1) * N]
                dy = across[c * N : (c + 1) * N, :N] + across[c * N : (c + 1) * N, N:]
                out_ref[c, z] += vs[h][c] - 0.5 * (vs[h][0] * dx + vs[h][1] * dy)

    scatter_one(nx // many - 1, True)

    @pl.loop(1, ny)
    def _(i):
        other = lax.rem(gy + i, ny)
        out_y(other, gy).wait_send()
        back_y(other, gy).wait_send()

    @pl.loop(0, sx)
    def _(i):
        other = lax.rem(gx + i, sx)

        @pl.when(other != gx)
        def _():
            out_x(other, gx).wait_send()

    @pl.when(gx < sx)
    def _():
        @pl.loop(1, nx)
        def _(i):
            back_x(lax.rem(gx + i, nx), gx).wait_send()

    @pl.loop(1, nx)
    def _(i):
        out_m(lax.rem(gx + i, nx), gx).wait_send()

    @pl.when(gx < nx - 1)
    def _():
        edge_low().wait_send()

    @pl.when(gx > 0)
    def _():
        edge_high().wait_send()

    for h in range(2):
        for r in range(2):
            for store in stores(h, r):
                store.wait()


def finish_kernel(src, dst, held, load_sem, store_sem):
    spots = [(c, pl.ds(4 * i, 4)) for c in range(3) for i in range(4)]
    loads = [pltpu.make_async_copy(src.at[p], held.at[p], load_sem.at[i]) for i, p in enumerate(spots)]
    stores = [pltpu.make_async_copy(held.at[p], dst.at[p], store_sem.at[i]) for i, p in enumerate(spots)]
    for load in loads:
        load.start()
    for load, store in zip(loads, stores):
        load.wait()
        store.start()
    for store in stores:
        store.wait()


def local(nx, ny, velocity, inv_x, inv_y, spike_x, spike_y, marker_force, marker_kernel, marker_owner, marker_row):
    depth = velocity.shape[1]
    half = depth // 2
    slots = marker_row.shape[0]
    args = (velocity, inv_x, inv_y, spike_x.T, spike_y.T, marker_force, marker_kernel,
            marker_owner.reshape(slots // N, N), marker_row.reshape(slots // N, N))
    sx, sy = min(depth, nx), min(depth, ny)
    dma, vmem = pltpu.SemaphoreType.DMA, pltpu.VMEM
    result = pl.pallas_call(
        functools.partial(whole_kernel, nx, ny),
        out_shape=jax.ShapeDtypeStruct(velocity.shape, F32),
        in_specs=[pl.BlockSpec(memory_space=pl.ANY)] * len(args),
        out_specs=pl.BlockSpec(memory_space=pl.ANY),
        scratch_shapes=[vmem(a.shape, a.dtype) for a in args] + [
            dma((len(args),)),
            vmem((slots, 2 * N), BF16),
            vmem((8, slots), F32),
            vmem((nx, BLOCK, N), BF16),
            vmem((nx, BLOCK, N), BF16),
            vmem((depth, 8, N), F32),
            vmem((depth, 3, 8, N), F32),
            vmem((3 * N, N), F32),
            vmem((2, depth, 8, N), F32),
            vmem((depth, 8, N), F32),
            vmem((depth, 8, N), F32),
            vmem((depth, 8, N), F32),
            vmem((depth, 3, 8, N), F32),
            vmem((nx, depth // sx, 8, N), F32),
            vmem((ny, depth // sy, 3, 8, N), F32),
            vmem((nx, depth // sx, 8, N), F32),
            vmem((ny, depth // sy, 3, 8, N), F32),
            vmem((nx // 4 * CAP, 6 * N), BF16),
            vmem((half * N, nx // 4 * CAP), BF16),
            vmem((2 * N, 2 * N), BF16),
            vmem((6 * N, N), BF16),
            vmem((2 * N, 2 * N), BF16),
            vmem((2 * N, 2 * N), BF16),
            vmem((3 * N, 2 * N), BF16),
            dma((nx,)), dma((nx,)), dma((sx,)), dma((nx,)), dma((ny,)), dma((ny,)),
            dma((nx,)), dma((sx,)), dma((ny,)), dma((ny,)), dma((2,)), dma((2,)),
            vmem(velocity.shape, F32), dma((12,)),
        ],
        compiler_params=pltpu.CompilerParams(vmem_limit_bytes=56 * 1024 * 1024, collective_id=0, has_side_effects=True),
        name="section",
    )(*args)
    return pl.pallas_call(
        finish_kernel,
        out_shape=jax.ShapeDtypeStruct(velocity.shape, F32),
        in_specs=[pl.BlockSpec(memory_space=pl.ANY)],
        out_specs=pl.BlockSpec(memory_space=pl.ANY),
        scratch_shapes=[vmem(velocity.shape, F32), dma((12,)), dma((12,))],
        compiler_params=pltpu.CompilerParams(vmem_limit_bytes=60 * 1024 * 1024),
        name="finish",
    )(result)


def solution(mesh):
    return jax.shard_map(
        functools.partial(local, mesh.shape["gx"], mesh.shape["gy"]),
        mesh=mesh,
        in_specs=(
            P(None, None, "gx", "gy"),
            P("gx", None),
            P("gy", None),
            P("gx", None),
            P("gy", None),
            P(None, ("gx", "gy")),
            P(("gx", "gy"), None),
            P(("gx", "gy"), None),
            P(("gx", "gy")),
        ),
        out_specs=P(None, None, "gx", "gy"),
        check_vma=False,
    )
```

```python
import functools

import jax
import jax.numpy as jnp
from jax import lax
from jax.experimental import pallas as pl
from jax.experimental.pallas import tpu as pltpu
from jax.sharding import PartitionSpec as P

HIGH = lax.Precision.HIGHEST
MESH = pl.DeviceIdType.MESH
F32, BF16 = jnp.float32, jnp.bfloat16
N = 128
CAP = 128
BLOCK = CAP + 16
NEAR, FAR = 7.0 / 9.0, 1.0 / 36.0


def iota(shape, dim):
    return lax.broadcasted_iota(jnp.int32, shape, dim)


def mm(a, b):
    return jnp.dot(a, b, preferred_element_type=F32)


def mm_nt(a, b, precision=None):
    return lax.dot_general(a, b, (((1,), (1,)), ((), ())), precision=precision, preferred_element_type=F32)


def split(a):
    hi = a.astype(BF16)
    return hi, (a - hi.astype(F32)).astype(BF16)


def inner_stencil(cell, row):
    gap = cell - row
    return jnp.where(gap == 1, NEAR, 0.0) - jnp.where(gap == -1, NEAR, 0.0) + jnp.where(gap == 2, FAR, 0.0) - jnp.where(gap == -2, FAR, 0.0)


def outer_stencil(row, column, first):
    which = column - first
    low2 = jnp.where((which == 0) & (row == 0), -FAR, 0.0)
    low1 = jnp.where((which == 1) & (row == 0), -NEAR, 0.0) + jnp.where((which == 1) & (row == 1), -FAR, 0.0)
    high1 = jnp.where((which == 2) & (row == N - 1), NEAR, 0.0) + jnp.where((which == 2) & (row == N - 2), FAR, 0.0)
    high2 = jnp.where((which == 3) & (row == N - 1), FAR, 0.0)
    return low2 + low1 + high1 + high2


def last_rows(inverse, spike_t):
    sub, lane = iota((N, N), 0), iota((N, N), 1)
    inner_t = inner_stencil(sub, lane)
    spread = [
        mm_nt(inner_t, jnp.broadcast_to(inverse[N - 2 + a : N - 1 + a, :], (N, N)), HIGH) for a in range(2)
    ]
    outer = jnp.dot(inverse[N - 8 :, :], outer_stencil(sub, lane, 0), precision=HIGH, preferred_element_type=F32)
    part, column = iota((2, N), 0), iota((2, N), 1)
    place = iota((1, N), 1)
    rows = []
    for a in range(2):
        row = outer[6 + a : 7 + a, :]
        for b in range(2):
            picked = jnp.where((part == b) & (column == N - 2 + a), spike_t, 0.0)
            value = jnp.sum(jnp.sum(picked, axis=1, keepdims=True), axis=0, keepdims=True)
            row = row + jnp.where(place == 4 + b, value, 0.0)
        rows.append(row)
    return spread, rows


def chain_y(count, got, reply):
    zero = jnp.zeros(got.shape[1:3] + (1, N), F32)

    def one(d, carry):
        s0, s1, low2, low1 = carry
        here = got[d]
        after = got[jnp.minimum(d + 1, count - 1)]
        more = (d + 1 < count).astype(F32)
        high1, high2 = after[:, :, 2:3, :] * more, after[:, :, 3:4, :] * more
        reply[d] = jnp.concatenate([s0, s1, low2, low1, high1, high2, zero, zero], axis=2)
        new = []
        for a in range(2):
            weight = here[:, :, 6 + a : 7 + a, :]
            total = here[:, :, a : a + 1, :]
            for k, value in enumerate((low2, low1, high1, high2, s0, s1)):
                total = total + weight[:, :, :, k : k + 1] * value
            new.append(total)
        return new[0], new[1], here[:, :, 4:5, :], here[:, :, 5:6, :]

    lax.fori_loop(0, count, one, (zero, zero, zero, zero), unroll=2)


def columns_x(spike_t, inverse):
    sub, lane = iota((N, N), 0), iota((N, N), 1)
    turn = lane % 32
    outer = jnp.dot(inverse, outer_stencil(sub, turn // 4, 2), precision=HIGH, preferred_element_type=F32)
    order = sub % 32 // 4
    spikes = jnp.where(order == 0, spike_t[0:1], jnp.where(order == 1, spike_t[1:2], 0.0)).T
    return outer + spikes


def columns_y(spike_t, inverse):
    sub, lane = iota((N, N), 0), iota((N, N), 1)
    outer = jnp.dot(inverse, outer_stencil(sub, lane % 8, 2), precision=HIGH, preferred_element_type=F32)
    order = sub % 8
    spikes = jnp.where(order == 0, spike_t[0:1], jnp.where(order == 1, spike_t[1:2], 0.0)).T
    return outer + spikes


def inner(inverse):
    sub, lane = iota((N, N), 0), iota((N, N), 1)
    return jnp.dot(inverse, inner_stencil(lane, sub), precision=HIGH, preferred_element_type=F32)


def chain_x(count, got, reply):
    real = iota((1, 4, N), 1) < 3
    zero = jnp.zeros((got.shape[1], 4, N), F32)

    def one(d, carry):
        s0, s1 = carry
        here = got[d]
        reply[d] = jnp.concatenate([s0, s1], axis=1)
        new = []
        for a in range(2):
            weight = here[0:1, 4 * a + 3 : 4 * a + 4, :]
            part = jnp.where(real, here[:, 4 * a : 4 * a + 4, :], 0.0)
            new.append(part + weight[:, :, 4:5] * s0 + weight[:, :, 5:6] * s1)
        return tuple(new)

    lax.fori_loop(0, count, one, (zero, zero), unroll=min(count, 8))


def whole_kernel(nx, ny, v_hbm, ix_hbm, iy_hbm, wx_hbm, wy_hbm, f_hbm, k_hbm, own_hbm, row_hbm, out_ref,
                 v_ref, ix_ref, iy_ref, wx_ref, wy_ref, f_ref, k_ref, own_ref, row_ref, load_sem,
                 wide_ref, pos_ref, mk_ref, got_mk, qx_ref, my_ref, line_ref,
                 edge_ref, low_ref, high_ref, ex_ref, ey_ref, got_x, got_y, reply_x, reply_y,
                 tile_ref, pick_ref, left_x, left_ex, right_y, right_ey, ext_y,
                 send_m, recv_m, send_x, recv_x, send_y, recv_y,
                 back_send_x, back_recv_x, back_send_y, back_recv_y, edge_send, edge_recv):
    gx, gy = lax.axis_index("gx"), lax.axis_index("gy")
    depth = v_ref.shape[1]
    half = depth // 2
    sx, sy = min(depth, nx), min(depth, ny)
    zx, zy = depth // sx, depth // sy
    chunks = own_ref.shape[0]
    per = 4
    rounds = nx // per
    sub, lane = iota((N, N), 0), iota((N, N), 1)

    pairs = [(own_hbm, own_ref), (row_hbm, row_ref), (f_hbm, f_ref), (k_hbm, k_ref), (v_hbm, v_ref),
             (ix_hbm, ix_ref), (iy_hbm, iy_ref), (wx_hbm, wx_ref), (wy_hbm, wy_ref)]
    loads = [pltpu.make_async_copy(src, dst, load_sem.at[i]) for i, (src, dst) in enumerate(pairs)]
    for load in loads:
        load.start()

    barrier = pltpu.get_barrier_semaphore()

    @pl.loop(1, nx)
    def _(i):
        pl.semaphore_signal(barrier, inc=1, device_id=(lax.rem(gx + i, nx), gy), device_id_type=MESH)

    @pl.loop(1, ny)
    def _(i):
        pl.semaphore_signal(barrier, inc=1, device_id=(gx, lax.rem(gy + i, ny)), device_id_type=MESH)

    def remote(src, dst, send, recv, to):
        return pltpu.make_async_remote_copy(
            src_ref=src, dst_ref=dst, send_sem=send, recv_sem=recv, device_id=to, device_id_type=MESH)

    def out_x(to, origin):
        return remote(qx_ref.at[pl.ds(to * zx, zx)], got_x.at[origin], send_x.at[to], recv_x.at[origin], (to, gy))

    def out_y(to, origin):
        return remote(my_ref.at[pl.ds(to * zy, zy)], got_y.at[origin], send_y.at[to], recv_y.at[origin], (gx, to))

    def out_m(to, origin):
        return remote(mk_ref.at[to], got_mk.at[origin], send_m.at[to], recv_m.at[origin], (to, gy))

    def back_x(to, origin):
        return remote(reply_x.at[to], ex_ref.at[pl.ds(origin * zx, zx)], back_send_x.at[to], back_recv_x.at[origin], (to, gy))

    def back_y(to, origin):
        return remote(reply_y.at[to], ey_ref.at[pl.ds(origin * zy, zy)], back_send_y.at[to], back_recv_y.at[origin], (gx, to))

    def edge_low():
        return remote(edge_ref.at[1], low_ref, edge_send.at[0], edge_recv.at[0], (jnp.minimum(gx + 1, nx - 1), gy))

    def edge_high():
        return remote(edge_ref.at[0], high_ref, edge_send.at[1], edge_recv.at[1], (jnp.maximum(gx - 1, 0), gy))

    for load in loads[:4]:
        load.wait()
    upto = jnp.concatenate([(sub <= lane).astype(BF16), jnp.ones((N, N), BF16)], axis=1)
    name = iota((nx, N), 0)
    before = jnp.zeros((nx, N), F32)
    for k in range(chunks):
        owner = own_ref[k : k + 1, :]
        hit = name == owner
        counted = mm(hit.astype(F32).astype(BF16), upto)
        rank = counted[:, :N] + before - 1.0
        before = before + counted[:, N:]
        place = jnp.sum(jnp.where(hit, rank, 0.0), axis=0, keepdims=True)
        pos_ref[0:1, k * N : (k + 1) * N] = owner.astype(F32)
        pos_ref[1:2, k * N : (k + 1) * N] = place

        cell = row_ref[k : k + 1, :]
        plane = cell // N
        upper = plane >= half
        three = f_ref[:, k * N : (k + 1) * N].astype(F32)
        facts = jnp.concatenate(
            [jnp.where(upper, 0.0, three), jnp.where(upper, three, 0.0),
             (plane % half).astype(F32), (cell % N).astype(F32)],
            axis=0,
        )
        wide_ref[k * N : (k + 1) * N, 0:N] = k_ref[k * N : (k + 1) * N, :]
        wide_ref[k * N : (k + 1) * N, N:] = jnp.tile(facts, (N // 8, 1)).T.astype(BF16)

    for load in loads[4:]:
        load.wait()
    blank = jnp.zeros((depth, 1, N), F32)
    for e, first in enumerate((0, N - 2)):
        edge_ref[e] = jnp.concatenate(
            [p for a in range(2) for p in [v_ref[c, :, first + a : first + a + 1, :] for c in range(3)] + [blank]], axis=1)

    pl.semaphore_wait(barrier, nx + ny - 2)

    @pl.when(gx < nx - 1)
    def _():
        edge_low().start()

    @pl.when(gx > 0)
    def _():
        edge_high().start()

    slot = iota((CAP, 1), 0).astype(F32).astype(BF16)

    def compact(low, high):
        @pl.loop(low, high)
        def _(step):
            owner, place = pos_ref[0:1, :], pos_ref[1:2, :]
            picks = []
            for i in range(per):
                to = lax.rem(gx + step * per + i, nx)
                mine = jnp.where(owner == to.astype(F32), place, -1.0).astype(BF16)
                picks.append(jnp.where(mine == slot, jnp.ones((), BF16), jnp.zeros((), BF16)))
            rows = mm(jnp.concatenate(picks, axis=0), wide_ref[...])
            for i in range(per):
                off = step * per + i
                to = lax.rem(gx + off, nx)
                part = rows[i * CAP : (i + 1) * CAP]
                mk_ref[to, 0:CAP, :] = part[:, :N].astype(BF16)
                facts_t = part[:, N:].T[0:8, :]
                mk_ref[to, CAP:, :] = jnp.concatenate([facts_t, jnp.zeros((8, N), F32)], axis=0).astype(BF16)

                @pl.when(off > 0)
                def _():
                    out_m(to, gx).start()

                @pl.when(off == 0)
                def _():
                    got_mk[gx] = mk_ref[gx]

    cuts = (0, max(1, rounds // 4), max(1, 3 * rounds // 4), rounds)
    compact(cuts[0], cuts[1])

    (sy0, sy1), (cy0, cy1) = last_rows(iy_ref[...], wy_ref[...])
    kind = lane % 8
    base = jnp.where(kind == 0, sy0, jnp.where(kind == 1, sy1, 0.0))
    for i, cell in enumerate((0, 1, N - 2, N - 1)):
        base = base + jnp.where((kind == 2 + i) & (sub == cell), 1.0, 0.0)
    base_hi, base_lo = (p.astype(F32) for p in split(base))
    line_ref[...] = jnp.zeros_like(line_ref)

    @pl.loop(0, depth)
    def _(z):
        mine = lane // 8 == z
        hi = jnp.where(mine, base_hi, 0.0).astype(BF16)
        lo = jnp.where(mine, base_lo, 0.0).astype(BF16)
        v_hi, v_lo = split(v_ref[:, z].reshape(3 * N, N))
        line_ref[...] += mm(jnp.concatenate([v_hi, v_lo], axis=1), jnp.concatenate([hi, hi], axis=0)) + mm(v_hi, lo)

    kind_row = sub % 8
    for c in range(3):
        lines = line_ref[c * N : (c + 1) * N, :].T
        lines = jnp.where(kind_row == 6, cy0, jnp.where(kind_row == 7, cy1, lines))
        my_ref[:, c] = lines.reshape(depth, 8, N)

    @pl.loop(1, ny)
    def _(i):
        out_y(lax.rem(gy + i, ny), gy).start()

    (sx0, sx1), (cx0, cx1) = last_rows(ix_ref[...], wx_ref[...])

    @pl.loop(0, depth)
    def _(z):
        rows = []
        for weight, known in ((sx0, cx0), (sx1, cx1)):
            rows += [jnp.sum(v_ref[c, z] * weight, axis=0, keepdims=True) for c in range(3)] + [known]
        qx_ref[z] = jnp.concatenate(rows, axis=0)

    @pl.when(gx == 0)
    def _():
        low_ref[...] = jnp.zeros_like(low_ref)

    @pl.when(gx == nx - 1)
    def _():
        high_ref[...] = jnp.zeros_like(high_ref)

    @pl.when(gx > 0)
    def _():
        edge_low().wait_recv()

    @pl.when(gx < nx - 1)
    def _():
        edge_high().wait_recv()

    outer = [low_ref[:, 0:4], low_ref[:, 4:8], high_ref[:, 0:4], high_ref[:, 4:8]]
    for a, known in ((0, cx0), (1, cx1)):
        total = qx_ref[:, 4 * a : 4 * a + 4]
        for k in range(4):
            total = total + known[:, k : k + 1].reshape(1, 1, 1) * outer[k]
        qx_ref[:, 4 * a : 4 * a + 4] = total

    @pl.loop(0, sx)
    def _(i):
        to = lax.rem(gx + i, sx)

        @pl.when(to != gx)
        def _():
            out_x(to, gx).start()

    compact(cuts[1], cuts[2])

    many, few = nx // 4, max(1, nx // 8)
    choice = jnp.full((), 0.5, BF16)

    def scatter_one(first, many):
        facts = []
        for i in range(many):
            off = first + i
            source = lax.rem(gx + nx - off, nx)

            @pl.when(off > 0)
            def _():
                out_m(gx, source).wait_recv()

            facts.append(got_mk[source, CAP:, :].astype(F32)[0:8])
        stack = jnp.concatenate(facts, axis=0)
        columns = jnp.tile(stack, (N // (8 * many), 1)).T.astype(BF16)
        for i in range(many):
            source = lax.rem(gx + nx - (first + i), nx)
            rows = got_mk[source, 0:CAP, :]
            for k in range(6):
                tile_ref[i * CAP : (i + 1) * CAP, k * N : (k + 1) * N] = rows * columns[:, 8 * i + k : 8 * i + k + 1]
            for zz in range(half):
                mine = jnp.where(facts[i][6:7] == float(zz), facts[i][7:8], -1.0).astype(BF16)
                pick_ref[zz * N : (zz + 1) * N, i * CAP : (i + 1) * CAP] = jnp.where(mine == slot, choice, jnp.zeros((), BF16))
        for h in range(2):
            for r in range(2):
                count = half // 2
                more = mm(pick_ref[r * count * N : (r + 1) * count * N, 0 : many * CAP], tile_ref[0 : many * CAP, h * 3 * N : (h + 1) * 3 * N])
                for c in range(3):
                    at = slice(h * half + r * count, h * half + (r + 1) * count)
                    out_ref[c, at] += more[:, c * N : (c + 1) * N].reshape(count, N, N)

    def scatter(low, high):
        @pl.loop(low, high)
        def _(step):
            scatter_one(step * many, many)

    hi, lo = split(inner(ix_ref[...]))
    left_x[0:N, 0:N], left_x[0:N, N:] = hi, hi
    left_x[N:, 0:N], left_x[N:, N:] = lo, lo
    cols = columns_x(wx_ref[...], ix_ref[...])
    for c in range(3):
        hi, lo = split(jnp.where(lane % 4 == c, cols, 0.0))
        left_ex[2 * c * N : (2 * c + 1) * N], left_ex[(2 * c + 1) * N : (2 * c + 2) * N] = hi, lo
    hi, lo = split(inner(iy_ref[...]).T)
    right_y[0:N, 0:N], right_y[0:N, N:] = hi, lo
    right_y[N:, 0:N], right_y[N:, N:] = hi, lo
    hi, lo = split(columns_y(wy_ref[...], iy_ref[...]).T)
    right_ey[0:N, 0:N], right_ey[0:N, N:] = hi, lo
    right_ey[N:, 0:N], right_ey[N:, N:] = hi, lo

    @pl.loop(0, half)
    def _(step):
        zs = [step, step + half]
        vs = [[v_ref[c, z] for c in range(3)] for z in zs]
        parts = [[split(v) for v in line] for line in vs]
        wide = jnp.concatenate([jnp.concatenate([hi, lo], axis=0) for line in parts for hi, lo in line], axis=1)
        both = mm(left_x[...], wide)
        for h, z in enumerate(zs):
            tall = jnp.concatenate([jnp.concatenate([hi, lo], axis=1) for hi, lo in parts[h]], axis=0)
            across = mm(tall, right_y[...])
            for c in range(3):
                k = h * 3 + c
                dx = both[:N, k * N : (k + 1) * N] + both[N:, k * N : (k + 1) * N]
                dy = across[c * N : (c + 1) * N, :N] + across[c * N : (c + 1) * N, N:]
                out_ref[c, z] = vs[h][c] - 0.5 * (vs[h][0] * dx + vs[h][1] * dy)

    got_y[gy] = my_ref[pl.ds(gy * zy, zy)]

    @pl.loop(1, ny)
    def _(i):
        out_y(gy, lax.rem(gy + i, ny)).wait_recv()

    chain_y(ny, got_y, reply_y)

    @pl.loop(1, ny)
    def _(i):
        back_y(lax.rem(gy + i, ny), gy).start()

    ey_ref[pl.ds(gy * zy, zy)] = reply_y[gy]

    @pl.when(gx < sx)
    def _():
        got_x[gx] = qx_ref[pl.ds(gx * zx, zx)]

        @pl.loop(1, nx)
        def _(i):
            out_x(gx, lax.rem(gx + i, nx)).wait_recv()

        chain_x(nx, got_x, reply_x)

        @pl.loop(1, nx)
        def _(i):
            back_x(lax.rem(gx + i, nx), gx).start()

        ex_ref[pl.ds(gx * zx, zx)] = reply_x[gx]

    compact(cuts[2], cuts[3])

    scatter(0, 3)

    @pl.loop(1, ny)
    def _(i):
        back_y(gy, lax.rem(gy + i, ny)).wait_recv()

    @pl.loop(0, sx)
    def _(i):
        other = lax.rem(gx + i, sx)

        @pl.when(other != gx)
        def _():
            back_x(gx, other).wait_recv()

    for c in range(3):
        hi, lo = split(ey_ref[:, c].reshape(8 * depth, N).T)
        ext_y[c * N : (c + 1) * N, 0:N], ext_y[c * N : (c + 1) * N, N:] = hi, lo

    @pl.loop(0, half)
    def _(step):
        zs = [step, step + half]
        ends = []
        for z in zs:
            hi, lo = split(jnp.concatenate([ex_ref[z], low_ref[z], high_ref[z], jnp.zeros((8, N), F32)], axis=0))
            ends.append(jnp.concatenate([hi, lo], axis=0))
        bent = mm(left_ex[:, 0:64], jnp.concatenate(ends, axis=1))
        for h, z in enumerate(zs):
            mine = iota((2 * N, 2 * N), 0) % N // 8 == z
            across = mm(ext_y[...], jnp.where(mine, right_ey[...].astype(F32), 0.0).astype(BF16))
            for c in range(3):
                dx = bent[2 * c * N : (2 * c + 1) * N, h * N : (h + 1) * N] + bent[(2 * c + 1) * N : (2 * c + 2) * N, h * N : (h + 1) * N]
                dy = across[c * N : (c + 1) * N, :N] + across[c * N : (c + 1) * N, N:]
                out_ref[c, z] -= 0.5 * (v_ref[0, z] * dx + v_ref[1, z] * dy)

    for first in range(3 * many, nx, few):
        scatter_one(first, few)

    @pl.loop(1, ny)
    def _(i):
        other = lax.rem(gy + i, ny)
        out_y(other, gy).wait_send()
        back_y(other, gy).wait_send()

    @pl.loop(0, sx)
    def _(i):
        other = lax.rem(gx + i, sx)

        @pl.when(other != gx)
        def _():
            out_x(other, gx).wait_send()

    @pl.when(gx < sx)
    def _():
        @pl.loop(1, nx)
        def _(i):
            back_x(lax.rem(gx + i, nx), gx).wait_send()

    @pl.loop(1, nx)
    def _(i):
        out_m(lax.rem(gx + i, nx), gx).wait_send()

    @pl.when(gx < nx - 1)
    def _():
        edge_low().wait_send()

    @pl.when(gx > 0)
    def _():
        edge_high().wait_send()


def local(nx, ny, velocity, inv_x, inv_y, spike_x, spike_y, marker_force, marker_kernel, marker_owner, marker_row):
    depth = velocity.shape[1]
    half = depth // 2
    slots = marker_row.shape[0]
    args = (velocity, inv_x, inv_y, spike_x.T, spike_y.T, marker_force, marker_kernel,
            marker_owner.reshape(slots // N, N), marker_row.reshape(slots // N, N))
    sx, sy = min(depth, nx), min(depth, ny)
    dma, vmem = pltpu.SemaphoreType.DMA, pltpu.VMEM
    return pl.pallas_call(
        functools.partial(whole_kernel, nx, ny),
        out_shape=vmem(velocity.shape, F32),
        in_specs=[pl.BlockSpec(memory_space=pl.ANY)] * len(args),
        out_specs=pl.BlockSpec(memory_space=vmem),
        scratch_shapes=[vmem(a.shape, a.dtype) for a in args] + [
            dma((len(args),)),
            vmem((slots, 2 * N), BF16),
            vmem((8, slots), F32),
            vmem((nx, BLOCK, N), BF16),
            vmem((nx, BLOCK, N), BF16),
            vmem((depth, 8, N), F32),
            vmem((depth, 3, 8, N), F32),
            vmem((3 * N, N), F32),
            vmem((2, depth, 8, N), F32),
            vmem((depth, 8, N), F32),
            vmem((depth, 8, N), F32),
            vmem((depth, 8, N), F32),
            vmem((depth, 3, 8, N), F32),
            vmem((nx, depth // sx, 8, N), F32),
            vmem((ny, depth // sy, 3, 8, N), F32),
            vmem((nx, depth // sx, 8, N), F32),
            vmem((ny, depth // sy, 3, 8, N), F32),
            vmem((nx // 4 * CAP, 6 * N), BF16),
            vmem((half * N, nx // 4 * CAP), BF16),
            vmem((2 * N, 2 * N), BF16),
            vmem((6 * N, N), BF16),
            vmem((2 * N, 2 * N), BF16),
            vmem((2 * N, 2 * N), BF16),
            vmem((3 * N, 2 * N), BF16),
            dma((nx,)), dma((nx,)), dma((sx,)), dma((nx,)), dma((ny,)), dma((ny,)),
            dma((nx,)), dma((sx,)), dma((ny,)), dma((ny,)), dma((2,)), dma((2,)),
        ],
        compiler_params=pltpu.CompilerParams(vmem_limit_bytes=56 * 1024 * 1024, collective_id=0, has_side_effects=True),
        name="section",
    )(*args)

def solution(mesh):
    return jax.shard_map(
        functools.partial(local, mesh.shape["gx"], mesh.shape["gy"]),
        mesh=mesh,
        in_specs=(
            P(None, None, "gx", "gy"),
            P("gx", None),
            P("gy", None),
            P("gx", None),
            P("gy", None),
            P(None, ("gx", "gy")),
            P(("gx", "gy"), None),
            P(("gx", "gy"), None),
            P(("gx", "gy")),
        ),
        out_specs=P(None, None, "gx", "gy"),
        check_vma=False,
    )
```

```python
import functools

import jax
import jax.numpy as jnp
from jax import lax
from jax.experimental import pallas as pl
from jax.experimental.pallas import tpu as pltpu
from jax.sharding import PartitionSpec as P

HIGH = lax.Precision.HIGHEST
MESH = pl.DeviceIdType.MESH
F32, BF16 = jnp.float32, jnp.bfloat16
N = 128
CAP = 128
NEAR, FAR = 7.0 / 9.0, 1.0 / 36.0


def iota(shape, dim):
    return lax.broadcasted_iota(jnp.int32, shape, dim)


def mm(a, b):
    return jnp.dot(a, b, preferred_element_type=F32)


def mm_nt(a, b, precision=None):
    return lax.dot_general(a, b, (((1,), (1,)), ((), ())), precision=precision, preferred_element_type=F32)


def split(a):
    hi = a.astype(BF16)
    return hi, (a - hi.astype(F32)).astype(BF16)


def inner_stencil(cell, row):
    gap = cell - row
    return jnp.where(gap == 1, NEAR, 0.0) - jnp.where(gap == -1, NEAR, 0.0) + jnp.where(gap == 2, FAR, 0.0) - jnp.where(gap == -2, FAR, 0.0)


def outer_stencil(row, column, first):
    which = column - first
    low2 = jnp.where((which == 0) & (row == 0), -FAR, 0.0)
    low1 = jnp.where((which == 1) & (row == 0), -NEAR, 0.0) + jnp.where((which == 1) & (row == 1), -FAR, 0.0)
    high1 = jnp.where((which == 2) & (row == N - 1), NEAR, 0.0) + jnp.where((which == 2) & (row == N - 2), FAR, 0.0)
    high2 = jnp.where((which == 3) & (row == N - 1), FAR, 0.0)
    return low2 + low1 + high1 + high2


def last_rows(inverse, spike_t):
    sub, lane = iota((N, N), 0), iota((N, N), 1)
    inner_t = inner_stencil(sub, lane)
    spread = [
        mm_nt(inner_t, jnp.broadcast_to(inverse[N - 2 + a : N - 1 + a, :], (N, N)), HIGH) for a in range(2)
    ]
    outer = jnp.dot(inverse[N - 8 :, :], outer_stencil(sub, lane, 0), precision=HIGH, preferred_element_type=F32)
    part, column = iota((2, N), 0), iota((2, N), 1)
    place = iota((1, N), 1)
    rows = []
    for a in range(2):
        row = outer[6 + a : 7 + a, :]
        for b in range(2):
            picked = jnp.where((part == b) & (column == N - 2 + a), spike_t, 0.0)
            value = jnp.sum(jnp.sum(picked, axis=1, keepdims=True), axis=0, keepdims=True)
            row = row + jnp.where(place == 4 + b, value, 0.0)
        rows.append(row)
    return spread, rows


def chain_y(count, got, reply):
    zero = jnp.zeros(got.shape[1:3] + (1, N), F32)

    def one(d, carry):
        s0, s1, low2, low1 = carry
        here = got[d]
        after = got[jnp.minimum(d + 1, count - 1)]
        more = (d + 1 < count).astype(F32)
        high1, high2 = after[:, :, 2:3, :] * more, after[:, :, 3:4, :] * more
        reply[d] = jnp.concatenate([s0, s1, low2, low1, high1, high2, zero, zero], axis=2)
        new = []
        for a in range(2):
            weight = here[:, :, 6 + a : 7 + a, :]
            total = here[:, :, a : a + 1, :]
            for k, value in enumerate((low2, low1, high1, high2, s0, s1)):
                total = total + weight[:, :, :, k : k + 1] * value
            new.append(total)
        return new[0], new[1], here[:, :, 4:5, :], here[:, :, 5:6, :]

    lax.fori_loop(0, count, one, (zero, zero, zero, zero), unroll=2)


def columns_x(spike_t, inverse):
    sub, lane = iota((N, N), 0), iota((N, N), 1)
    turn = lane % 32
    outer = jnp.dot(inverse, outer_stencil(sub, turn // 4, 2), precision=HIGH, preferred_element_type=F32)
    order = sub % 32 // 4
    spikes = jnp.where(order == 0, spike_t[0:1], jnp.where(order == 1, spike_t[1:2], 0.0)).T
    return outer + spikes


def columns_y(spike_t, inverse):
    sub, lane = iota((N, N), 0), iota((N, N), 1)
    outer = jnp.dot(inverse, outer_stencil(sub, lane % 8, 2), precision=HIGH, preferred_element_type=F32)
    order = sub % 8
    spikes = jnp.where(order == 0, spike_t[0:1], jnp.where(order == 1, spike_t[1:2], 0.0)).T
    return outer + spikes


def inner(inverse):
    sub, lane = iota((N, N), 0), iota((N, N), 1)
    return jnp.dot(inverse, inner_stencil(lane, sub), precision=HIGH, preferred_element_type=F32)


def chain_x(count, got, reply):
    real = iota((1, 4, N), 1) < 3
    zero = jnp.zeros((got.shape[1], 4, N), F32)

    def one(d, carry):
        s0, s1 = carry
        here = got[d]
        reply[d] = jnp.concatenate([s0, s1], axis=1)
        new = []
        for a in range(2):
            weight = here[0:1, 4 * a + 3 : 4 * a + 4, :]
            part = jnp.where(real, here[:, 4 * a : 4 * a + 4, :], 0.0)
            new.append(part + weight[:, :, 4:5] * s0 + weight[:, :, 5:6] * s1)
        return tuple(new)

    lax.fori_loop(0, count, one, (zero, zero), unroll=min(count, 8))


def whole_kernel(nx, ny, v_hbm, ix_hbm, iy_hbm, wx_hbm, wy_hbm, f_hbm, k_hbm, own_hbm, row_hbm, out_ref,
                 v_ref, ix_ref, iy_ref, wx_ref, wy_ref, f_ref, k_ref, own_ref, row_ref, load_sem,
                 wide_ref, pos_ref, mk_ref, got_mk, qx_ref, my_ref, line_ref,
                 edge_ref, low_ref, high_ref, ex_ref, ey_ref, got_x, got_y, reply_x, reply_y,
                 tile_ref, pick_ref, left_x, left_ex, right_y, right_ey, ext_y,
                 send_m, recv_m, send_x, recv_x, send_y, recv_y,
                 back_send_x, back_recv_x, back_send_y, back_recv_y, edge_send, edge_recv, mf_ref, got_mf, send_f, recv_f):
    gx, gy = lax.axis_index("gx"), lax.axis_index("gy")
    depth = v_ref.shape[1]
    half = depth // 2
    sx, sy = min(depth, nx), min(depth, ny)
    zx, zy = depth // sx, depth // sy
    chunks = own_ref.shape[0]
    per = 4
    rounds = nx // per
    sub, lane = iota((N, N), 0), iota((N, N), 1)

    pairs = [(own_hbm, own_ref), (row_hbm, row_ref), (f_hbm, f_ref), (k_hbm, k_ref), (v_hbm, v_ref),
             (ix_hbm, ix_ref), (iy_hbm, iy_ref), (wx_hbm, wx_ref), (wy_hbm, wy_ref)]
    loads = [pltpu.make_async_copy(src, dst, load_sem.at[i]) for i, (src, dst) in enumerate(pairs)]
    for load in loads:
        load.start()

    barrier = pltpu.get_barrier_semaphore()

    @pl.loop(1, nx)
    def _(i):
        pl.semaphore_signal(barrier, inc=1, device_id=(lax.rem(gx + i, nx), gy), device_id_type=MESH)

    @pl.loop(1, ny)
    def _(i):
        pl.semaphore_signal(barrier, inc=1, device_id=(gx, lax.rem(gy + i, ny)), device_id_type=MESH)

    def remote(src, dst, send, recv, to):
        return pltpu.make_async_remote_copy(
            src_ref=src, dst_ref=dst, send_sem=send, recv_sem=recv, device_id=to, device_id_type=MESH)

    def out_x(to, origin):
        return remote(qx_ref.at[pl.ds(to * zx, zx)], got_x.at[origin], send_x.at[to], recv_x.at[origin], (to, gy))

    def out_y(to, origin):
        return remote(my_ref.at[pl.ds(to * zy, zy)], got_y.at[origin], send_y.at[to], recv_y.at[origin], (gx, to))

    def out_m(to, origin):
        return remote(mk_ref.at[to], got_mk.at[origin], send_m.at[to], recv_m.at[origin], (to, gy))

    def out_f(to, origin):
        return remote(mf_ref.at[to], got_mf.at[origin], send_f.at[to], recv_f.at[origin], (to, gy))

    def back_x(to, origin):
        return remote(reply_x.at[to], ex_ref.at[pl.ds(origin * zx, zx)], back_send_x.at[to], back_recv_x.at[origin], (to, gy))

    def back_y(to, origin):
        return remote(reply_y.at[to], ey_ref.at[pl.ds(origin * zy, zy)], back_send_y.at[to], back_recv_y.at[origin], (gx, to))

    def edge_low():
        return remote(edge_ref.at[1], low_ref, edge_send.at[0], edge_recv.at[0], (jnp.minimum(gx + 1, nx - 1), gy))

    def edge_high():
        return remote(edge_ref.at[0], high_ref, edge_send.at[1], edge_recv.at[1], (jnp.maximum(gx - 1, 0), gy))

    for load in loads[:4]:
        load.wait()
    upto = jnp.concatenate([(sub <= lane).astype(BF16), jnp.ones((N, N), BF16)], axis=1)
    name = iota((nx, N), 0)
    before = jnp.zeros((nx, N), F32)
    for k in range(chunks):
        owner = own_ref[k : k + 1, :]
        hit = name == owner
        counted = mm(hit.astype(F32).astype(BF16), upto)
        rank = counted[:, :N] + before - 1.0
        before = before + counted[:, N:]
        place = jnp.sum(jnp.where(hit, rank, 0.0), axis=0, keepdims=True)
        pos_ref[0:1, k * N : (k + 1) * N] = owner.astype(F32)
        pos_ref[1:2, k * N : (k + 1) * N] = place

        cell = row_ref[k : k + 1, :]
        plane = cell // N
        three = f_ref[:, k * N : (k + 1) * N].astype(F32)
        facts = jnp.concatenate(
            [three, plane.astype(F32), (cell % N).astype(F32), jnp.zeros((3, N), F32)],
            axis=0,
        )
        wide_ref[k * N : (k + 1) * N, 0:N] = k_ref[k * N : (k + 1) * N, :]
        wide_ref[k * N : (k + 1) * N, N:] = jnp.tile(facts, (N // 8, 1)).T.astype(BF16)

    for load in loads[4:]:
        load.wait()
    blank = jnp.zeros((depth, 1, N), F32)
    for e, first in enumerate((0, N - 2)):
        edge_ref[e] = jnp.concatenate(
            [p for a in range(2) for p in [v_ref[c, :, first + a : first + a + 1, :] for c in range(3)] + [blank]], axis=1)

    pl.semaphore_wait(barrier, nx + ny - 2)

    @pl.when(gx < nx - 1)
    def _():
        edge_low().start()

    @pl.when(gx > 0)
    def _():
        edge_high().start()

    slot = iota((CAP, 1), 0).astype(F32).astype(BF16)

    def compact(low, high):
        @pl.loop(low, high)
        def _(step):
            owner, place = pos_ref[0:1, :], pos_ref[1:2, :]
            picks = []
            for i in range(per):
                to = lax.rem(gx + step * per + i, nx)
                mine = jnp.where(owner == to.astype(F32), place, -1.0).astype(BF16)
                picks.append(jnp.where(mine == slot, jnp.ones((), BF16), jnp.zeros((), BF16)))
            rows = mm(jnp.concatenate(picks, axis=0), wide_ref[...])
            for i in range(per):
                off = step * per + i
                to = lax.rem(gx + off, nx)
                part = rows[i * CAP : (i + 1) * CAP]
                mk_ref[to] = part[:, :N].astype(BF16)
                facts_t = part[:, N:].T
                mf_ref[to] = jnp.concatenate([facts_t[0:3], facts_t[3:4] * N + facts_t[4:5]], axis=0)

                @pl.when(off > 0)
                def _():
                    out_m(to, gx).start()
                    out_f(to, gx).start()

                @pl.when(off == 0)
                def _():
                    got_mk[gx] = mk_ref[gx]
                    got_mf[gx] = mf_ref[gx]

    cuts = (0, max(1, rounds // 4), max(1, 3 * rounds // 4), rounds)
    compact(cuts[0], cuts[1])

    (sy0, sy1), (cy0, cy1) = last_rows(iy_ref[...], wy_ref[...])
    kind = lane % 8
    base = jnp.where(kind == 0, sy0, jnp.where(kind == 1, sy1, 0.0))
    for i, cell in enumerate((0, 1, N - 2, N - 1)):
        base = base + jnp.where((kind == 2 + i) & (sub == cell), 1.0, 0.0)
    base_hi, base_lo = (p.astype(F32) for p in split(base))
    line_ref[...] = jnp.zeros_like(line_ref)

    @pl.loop(0, depth)
    def _(z):
        mine = lane // 8 == z
        hi = jnp.where(mine, base_hi, 0.0).astype(BF16)
        lo = jnp.where(mine, base_lo, 0.0).astype(BF16)
        v_hi, v_lo = split(v_ref[:, z].reshape(3 * N, N))
        line_ref[...] += mm(jnp.concatenate([v_hi, v_lo], axis=1), jnp.concatenate([hi, hi], axis=0)) + mm(v_hi, lo)

    kind_row = sub % 8
    for c in range(3):
        lines = line_ref[c * N : (c + 1) * N, :].T
        lines = jnp.where(kind_row == 6, cy0, jnp.where(kind_row == 7, cy1, lines))
        my_ref[:, c] = lines.reshape(depth, 8, N)

    @pl.loop(1, ny)
    def _(i):
        out_y(lax.rem(gy + i, ny), gy).start()

    (sx0, sx1), (cx0, cx1) = last_rows(ix_ref[...], wx_ref[...])

    @pl.loop(0, depth)
    def _(z):
        rows = []
        for weight, known in ((sx0, cx0), (sx1, cx1)):
            rows += [jnp.sum(v_ref[c, z] * weight, axis=0, keepdims=True) for c in range(3)] + [known]
        qx_ref[z] = jnp.concatenate(rows, axis=0)

    @pl.when(gx == 0)
    def _():
        low_ref[...] = jnp.zeros_like(low_ref)

    @pl.when(gx == nx - 1)
    def _():
        high_ref[...] = jnp.zeros_like(high_ref)

    @pl.when(gx > 0)
    def _():
        edge_low().wait_recv()

    @pl.when(gx < nx - 1)
    def _():
        edge_high().wait_recv()

    outer = [low_ref[:, 0:4], low_ref[:, 4:8], high_ref[:, 0:4], high_ref[:, 4:8]]
    for a, known in ((0, cx0), (1, cx1)):
        total = qx_ref[:, 4 * a : 4 * a + 4]
        for k in range(4):
            total = total + known[:, k : k + 1].reshape(1, 1, 1) * outer[k]
        qx_ref[:, 4 * a : 4 * a + 4] = total

    @pl.loop(0, sx)
    def _(i):
        to = lax.rem(gx + i, sx)

        @pl.when(to != gx)
        def _():
            out_x(to, gx).start()

    compact(cuts[1], cuts[2])

    many, few = nx // 4, max(1, nx // 8)
    choice = jnp.full((), 0.5, BF16)

    def scatter_one(first, many):
        facts, cells = [], []
        for i in range(many):
            off = first + i
            source = lax.rem(gx + nx - off, nx)

            @pl.when(off > 0)
            def _():
                out_m(gx, source).wait_recv()
                out_f(gx, source).wait_recv()

            got = got_mf[source]
            upper = got[3:4] >= float(half * N)
            facts += [jnp.where(upper, 0.0, got[0:3]), jnp.where(upper, got[0:3], 0.0), jnp.zeros((2, N), F32)]
            cells.append(jnp.where(upper, got[3:4] - float(half * N), got[3:4]))
        stack = jnp.concatenate(facts, axis=0)
        columns = jnp.tile(stack, (N // (8 * many), 1)).T.astype(BF16)
        for i in range(many):
            source = lax.rem(gx + nx - (first + i), nx)
            rows = got_mk[source]
            for k in range(6):
                tile_ref[i * CAP : (i + 1) * CAP, k * N : (k + 1) * N] = rows * columns[:, 8 * i + k : 8 * i + k + 1]
            for zz in range(half):
                x = cells[i] - float(zz * N)
                mine = jnp.where((x >= 0.0) & (x < float(N)), x, -1.0).astype(BF16)
                pick_ref[zz * N : (zz + 1) * N, i * CAP : (i + 1) * CAP] = jnp.where(mine == slot, choice, jnp.zeros((), BF16))
        for h in range(2):
            for r in range(2):
                count = half // 2
                more = mm(pick_ref[r * count * N : (r + 1) * count * N, 0 : many * CAP], tile_ref[0 : many * CAP, h * 3 * N : (h + 1) * 3 * N])
                for c in range(3):
                    at = slice(h * half + r * count, h * half + (r + 1) * count)
                    out_ref[c, at] += more[:, c * N : (c + 1) * N].reshape(count, N, N)

    def scatter(low, high):
        @pl.loop(low, high)
        def _(step):
            scatter_one(step * many, many)

    hi, lo = split(inner(ix_ref[...]))
    left_x[0:N, 0:N], left_x[0:N, N:] = hi, hi
    left_x[N:, 0:N], left_x[N:, N:] = lo, lo
    cols = columns_x(wx_ref[...], ix_ref[...])
    for c in range(3):
        hi, lo = split(jnp.where(lane % 4 == c, cols, 0.0))
        left_ex[2 * c * N : (2 * c + 1) * N], left_ex[(2 * c + 1) * N : (2 * c + 2) * N] = hi, lo
    hi, lo = split(inner(iy_ref[...]).T)
    right_y[0:N, 0:N], right_y[0:N, N:] = hi, lo
    right_y[N:, 0:N], right_y[N:, N:] = hi, lo
    hi, lo = split(columns_y(wy_ref[...], iy_ref[...]).T)
    right_ey[0:N, 0:N], right_ey[0:N, N:] = hi, lo
    right_ey[N:, 0:N], right_ey[N:, N:] = hi, lo

    @pl.loop(0, half)
    def _(step):
        zs = [step, step + half]
        vs = [[v_ref[c, z] for c in range(3)] for z in zs]
        parts = [[split(v) for v in line] for line in vs]
        wide = jnp.concatenate([jnp.concatenate([hi, lo], axis=0) for line in parts for hi, lo in line], axis=1)
        both = mm(left_x[...], wide)
        for h, z in enumerate(zs):
            tall = jnp.concatenate([jnp.concatenate([hi, lo], axis=1) for hi, lo in parts[h]], axis=0)
            across = mm(tall, right_y[...])
            for c in range(3):
                k = h * 3 + c
                dx = both[:N, k * N : (k + 1) * N] + both[N:, k * N : (k + 1) * N]
                dy = across[c * N : (c + 1) * N, :N] + across[c * N : (c + 1) * N, N:]
                out_ref[c, z] = vs[h][c] - 0.5 * (vs[h][0] * dx + vs[h][1] * dy)

    got_y[gy] = my_ref[pl.ds(gy * zy, zy)]

    @pl.loop(1, ny)
    def _(i):
        out_y(gy, lax.rem(gy + i, ny)).wait_recv()

    chain_y(ny, got_y, reply_y)

    @pl.loop(1, ny)
    def _(i):
        back_y(lax.rem(gy + i, ny), gy).start()

    ey_ref[pl.ds(gy * zy, zy)] = reply_y[gy]

    @pl.when(gx < sx)
    def _():
        got_x[gx] = qx_ref[pl.ds(gx * zx, zx)]

        @pl.loop(1, nx)
        def _(i):
            out_x(gx, lax.rem(gx + i, nx)).wait_recv()

        chain_x(nx, got_x, reply_x)

        @pl.loop(1, nx)
        def _(i):
            back_x(lax.rem(gx + i, nx), gx).start()

        ex_ref[pl.ds(gx * zx, zx)] = reply_x[gx]

    compact(cuts[2], cuts[3])

    scatter(0, 3)

    @pl.loop(1, ny)
    def _(i):
        back_y(gy, lax.rem(gy + i, ny)).wait_recv()

    @pl.loop(0, sx)
    def _(i):
        other = lax.rem(gx + i, sx)

        @pl.when(other != gx)
        def _():
            back_x(gx, other).wait_recv()

    for c in range(3):
        hi, lo = split(ey_ref[:, c].reshape(8 * depth, N).T)
        ext_y[c * N : (c + 1) * N, 0:N], ext_y[c * N : (c + 1) * N, N:] = hi, lo

    @pl.loop(0, half)
    def _(step):
        zs = [step, step + half]
        ends = []
        for z in zs:
            hi, lo = split(jnp.concatenate([ex_ref[z], low_ref[z], high_ref[z], jnp.zeros((8, N), F32)], axis=0))
            ends.append(jnp.concatenate([hi, lo], axis=0))
        bent = mm(left_ex[:, 0:64], jnp.concatenate(ends, axis=1))
        for h, z in enumerate(zs):
            mine = iota((2 * N, 2 * N), 0) % N // 8 == z
            across = mm(ext_y[...], jnp.where(mine, right_ey[...].astype(F32), 0.0).astype(BF16))
            for c in range(3):
                dx = bent[2 * c * N : (2 * c + 1) * N, h * N : (h + 1) * N] + bent[(2 * c + 1) * N : (2 * c + 2) * N, h * N : (h + 1) * N]
                dy = across[c * N : (c + 1) * N, :N] + across[c * N : (c + 1) * N, N:]
                out_ref[c, z] -= 0.5 * (v_ref[0, z] * dx + v_ref[1, z] * dy)

    for first in range(3 * many, nx, few):
        scatter_one(first, few)

    @pl.loop(1, ny)
    def _(i):
        other = lax.rem(gy + i, ny)
        out_y(other, gy).wait_send()
        back_y(other, gy).wait_send()

    @pl.loop(0, sx)
    def _(i):
        other = lax.rem(gx + i, sx)

        @pl.when(other != gx)
        def _():
            out_x(other, gx).wait_send()

    @pl.when(gx < sx)
    def _():
        @pl.loop(1, nx)
        def _(i):
            back_x(lax.rem(gx + i, nx), gx).wait_send()

    @pl.loop(1, nx)
    def _(i):
        out_m(lax.rem(gx + i, nx), gx).wait_send()
        out_f(lax.rem(gx + i, nx), gx).wait_send()

    @pl.when(gx < nx - 1)
    def _():
        edge_low().wait_send()

    @pl.when(gx > 0)
    def _():
        edge_high().wait_send()


def local(nx, ny, velocity, inv_x, inv_y, spike_x, spike_y, marker_force, marker_kernel, marker_owner, marker_row):
    depth = velocity.shape[1]
    half = depth // 2
    slots = marker_row.shape[0]
    args = (velocity, inv_x, inv_y, spike_x.T, spike_y.T, marker_force, marker_kernel,
            marker_owner.reshape(slots // N, N), marker_row.reshape(slots // N, N))
    sx, sy = min(depth, nx), min(depth, ny)
    dma, vmem = pltpu.SemaphoreType.DMA, pltpu.VMEM
    return pl.pallas_call(
        functools.partial(whole_kernel, nx, ny),
        out_shape=vmem(velocity.shape, F32),
        in_specs=[pl.BlockSpec(memory_space=pl.ANY)] * len(args),
        out_specs=pl.BlockSpec(memory_space=vmem),
        scratch_shapes=[vmem(a.shape, a.dtype) for a in args] + [
            dma((len(args),)),
            vmem((slots, 2 * N), BF16),
            vmem((8, slots), F32),
            vmem((nx, CAP, N), BF16),
            vmem((nx, CAP, N), BF16),
            vmem((depth, 8, N), F32),
            vmem((depth, 3, 8, N), F32),
            vmem((3 * N, N), F32),
            vmem((2, depth, 8, N), F32),
            vmem((depth, 8, N), F32),
            vmem((depth, 8, N), F32),
            vmem((depth, 8, N), F32),
            vmem((depth, 3, 8, N), F32),
            vmem((nx, depth // sx, 8, N), F32),
            vmem((ny, depth // sy, 3, 8, N), F32),
            vmem((nx, depth // sx, 8, N), F32),
            vmem((ny, depth // sy, 3, 8, N), F32),
            vmem((nx // 4 * CAP, 6 * N), BF16),
            vmem((half * N, nx // 4 * CAP), BF16),
            vmem((2 * N, 2 * N), BF16),
            vmem((6 * N, N), BF16),
            vmem((2 * N, 2 * N), BF16),
            vmem((2 * N, 2 * N), BF16),
            vmem((3 * N, 2 * N), BF16),
            dma((nx,)), dma((nx,)), dma((sx,)), dma((nx,)), dma((ny,)), dma((ny,)),
            dma((nx,)), dma((sx,)), dma((ny,)), dma((ny,)), dma((2,)), dma((2,)),
            vmem((nx, 4, N), F32), vmem((nx, 4, N), F32), dma((nx,)), dma((nx,)),
        ],
        compiler_params=pltpu.CompilerParams(vmem_limit_bytes=56 * 1024 * 1024, collective_id=0, has_side_effects=True),
        name="section",
    )(*args)

def solution(mesh):
    return jax.shard_map(
        functools.partial(local, mesh.shape["gx"], mesh.shape["gy"]),
        mesh=mesh,
        in_specs=(
            P(None, None, "gx", "gy"),
            P("gx", None),
            P("gy", None),
            P("gx", None),
            P("gy", None),
            P(None, ("gx", "gy")),
            P(("gx", "gy"), None),
            P(("gx", "gy"), None),
            P(("gx", "gy")),
        ),
        out_specs=P(None, None, "gx", "gy"),
        check_vma=False,
    )
```
